32 devices in a mesh: dp: 16 (over z, x, core), mp: 2 (over y).
Axes of the slice: x: 2, y: 2, z: 4, core: 2. Of those that a mesh axis runs over, the one named last changes fastest.
Arguments:
- hidden_in: bfloat16 [128, 64, 768], P('dp'), may hold values from -6 to 6
- image_feats: bfloat16 [128, 257, 1408], P('dp'), may hold values from -6 to 6
- caption_lengths: int32 [128, 3], P('dp'), may hold values from 1 to 16, 32 in all within a row
- pair_image: int32 [384], P('dp'), may hold values from 0 to 127, as said below
- out_grad: bfloat16 [128, 64, 768], P('dp'), may hold values from -6 to 6
- self_qkv: bfloat16 [3, 768, 768], P(None, 'dp', 'mp'), may hold values from -0.21875 to 0.21875
- self_out: bfloat16 [768, 768], P('mp', 'dp'), may hold values from -0.625 to 0.625
- cross_query: bfloat16 [768, 768], P('dp', 'mp'), may hold values from -0.21875 to 0.21875
- cross_kv: bfloat16 [2, 1408, 768], P(None, 'dp', 'mp'), may hold values from -0.15625 to 0.15625
- cross_out: bfloat16 [768, 768], P('mp', 'dp'), may hold values from -0.875 to 0.875
- up_weight: bfloat16 [768, 3072], P('dp', 'mp'), may hold values from -0.21875 to 0.21875
- down_weight: bfloat16 [3072, 768], P('mp', 'dp'), may hold values from -0.15625 to 0.15625
- vision_proj: bfloat16 [768, 256], P('dp'), may hold values from -0.21875 to 0.21875
- text_proj: bfloat16 [768, 256], P('dp'), may hold values from -0.21875 to 0.21875
- norm_gain: bfloat16 [3, 768], P(None, 'dp'), may hold values from 0.5 to 1.5
- norm_bias: bfloat16 [3, 768], P(None, 'dp'), may hold values from -2.5 to 2.5
Outputs:
- contrast_loss: float32 [], replicated
- block_out: bfloat16 [128, 64, 768], P('dp')
- grad_hidden: bfloat16 [128, 64, 768], P('dp')
- grad_feats: bfloat16 [128, 257, 1408], P('dp')
- grad_self_qkv: float32 [3, 768, 768], P(None, 'dp', 'mp')
- grad_self_out: float32 [768, 768], P('mp', 'dp')
- grad_cross_query: float32 [768, 768], P('dp', 'mp')
- grad_cross_kv: float32 [2, 1408, 768], P(None, 'dp', 'mp')
- grad_cross_out: float32 [768, 768], P('mp', 'dp')
- grad_up_weight: float32 [768, 3072], P('dp', 'mp')
- grad_down_weight: float32 [3072, 768], P('mp', 'dp')
- grad_vision_proj: float32 [768, 256], P('dp')
- grad_text_proj: float32 [768, 256], P('dp')
- grad_norm_gain: float32 [3, 768], P(None, 'dp')
- grad_norm_bias: float32 [3, 768], P(None, 'dp')
The draws below stay inside these ranges and needn't reach their ends.
Inputs may be any that keep to these rules, and one draw needn't show every extreme that they name: `caption_lengths`: in each item the 3 lengths sum to 32, and the largest is half of 32. `pair_image`: items 0 to 63 are each named by exactly one caption, the other items by exactly five.
All inputs are finite; a program needn't handle non-finite values.
Results may differ from the reference program's by a relative error of at most 0.02.
Values may be sent and summed in bfloat16 or wider, within the bound.
No kernel may reach another device: no remote copies, remote signals or barrier semaphores. Data moves between devices by JAX's collectives and lax.ppermute only.
A program may use at most 192 MiB of HBM per device.

```python
import math
import jax
import jax.numpy as jnp
import numpy as np
from jax import lax

HEADS = 12
HEAD_DIM = 64
D = 768
FF = 3072
DV = 1408
NV = 257
NQ = 32
EMB = 256
TXT = 32
CAPS = 3
S = 64
ITEMS = 128
NTXT = 384


def draw_pair_image(key, part):
    half_items = ITEMS // 2
    single = jnp.arange(half_items, dtype=jnp.int32)
    many = jnp.repeat(jnp.arange(half_items, ITEMS, dtype=jnp.int32), 5, total_repeat_length=5 * (ITEMS - half_items))
    listed = jnp.concatenate([single, many])
    order = jax.random.permutation(key, NTXT)
    return listed[order].astype(jnp.int32)


def block_levels(key, shape, shards, smallest, top_value):
    factor_of = 1.0
    for dim, parts in shards:
        steps = jax.random.uniform(jax.random.fold_in(jax.random.fold_in(key, 6), dim), (parts,), jnp.float32, smallest / len(shards), top_value / len(shards))
        factor_of = factor_of * jnp.repeat(jnp.exp(steps), shape[dim] // parts).reshape((-1,) + (1,) * (len(shape) - 1 - dim))
    return factor_of


def length_profile(number_of, total, bound, lean):
    weights = [(1 << 20) // math.isqrt(rank ** lean) + 1 for rank in range(2, number_of + 1)]
    rest, given = total - bound - (number_of - 1), [1] * (number_of - 1)
    while rest > 0:
        free = [i for i in range(number_of - 1) if given[i] < bound]
        pool, remaining = sum([weights[i] for i in free]), rest
        for i in free:
            extra = min(bound - given[i], max(1, remaining * weights[i] // pool), rest)
            given[i] = given[i] + extra
            rest = rest - extra
    return np.array([bound] + given)


def ragged(key, number_of, total, bound, skew):
    if number_of == 2:
        one = jax.random.randint(key, (), max(1, total - bound), min(bound, total - 1) + 1)
        return jnp.stack([one, total - one])
    sizes = jnp.asarray(length_profile(number_of, total, bound, skew), jnp.int32)
    twos = (number_of - 1) // 2
    source_of, taker = sizes[1:1 + 2 * twos:2], sizes[2:2 + 2 * twos:2]
    margin = jnp.minimum(source_of - 1, bound - taker)
    shifted = jax.random.randint(jax.random.fold_in(key, 1), (twos,), 0, 1 << 20) % (margin + 1)
    sizes = sizes.at[1:1 + 2 * twos:2].set(source_of - shifted).at[2:2 + 2 * twos:2].set(taker + shifted)
    return sizes[jax.random.permutation(jax.random.fold_in(key, 2), number_of)]


def scatter_about(key, dims, spread, bound, pieces=(), held_as=jnp.bfloat16):
    level = block_levels(key, dims, pieces, -0.22, 0.18) if pieces else 1.0
    result = jax.random.normal(key, dims, jnp.float32) * spread * level
    return jnp.minimum(jnp.maximum(result, -bound), bound).astype(held_as)


def setup_inputs(seed: int = 0) -> dict:
    arg_keys = jax.random.split(jax.random.key(seed), 17)
    return {
        "hidden_in": scatter_about(arg_keys[0], (ITEMS, S, D), 1.0, 6.0, ((0, 16),)),
        "image_feats": scatter_about(arg_keys[1], (ITEMS, NV, DV), 1.0, 6.0, ((0, 16),)),
        "caption_lengths": jax.vmap(lambda own: ragged(own, CAPS, TXT, TXT // 2, 0))(jax.random.split(arg_keys[2], ITEMS)).reshape((ITEMS, CAPS)).astype(jnp.int32),
        "pair_image": draw_pair_image(jax.random.fold_in(arg_keys[16], 71), 0),
        "out_grad": scatter_about(arg_keys[4], (ITEMS, S, D), 1.0, 6.0, ((0, 16),)),
        "self_qkv": scatter_about(arg_keys[5], (3, D, D), D ** -0.5, 0.21875, ((1, 16), (2, 2))),
        "self_out": scatter_about(arg_keys[6], (D, D), (D // 8) ** -0.5, 0.625, ((0, 2), (1, 16))),
        "cross_query": scatter_about(arg_keys[7], (D, D), D ** -0.5, 0.21875, ((0, 16), (1, 2))),
        "cross_kv": scatter_about(arg_keys[8], (2, DV, D), DV ** -0.5, 0.15625, ((1, 16), (2, 2))),
        "cross_out": scatter_about(arg_keys[9], (D, D), (D // 16) ** -0.5, 0.875, ((0, 2), (1, 16))),
        "up_weight": scatter_about(arg_keys[10], (D, FF), D ** -0.5, 0.21875, ((0, 16), (1, 2))),
        "down_weight": scatter_about(arg_keys[11], (FF, D), (FF // 2) ** -0.5, 0.15625, ((0, 2), (1, 16))),
        "vision_proj": scatter_about(arg_keys[12], (D, EMB), D ** -0.5, 0.21875, ((0, 16),)),
        "text_proj": scatter_about(arg_keys[13], (D, EMB), D ** -0.5, 0.21875, ((0, 16),)),
        "norm_gain": jnp.clip(1.0 + 0.1 * jax.random.normal(arg_keys[14], (3, D), jnp.float32), 0.5, 1.5).astype(jnp.bfloat16),
        "norm_bias": scatter_about(arg_keys[15], (3, D), 0.3, 2.5, ((1, 16),)),
    }


@jax.custom_vjp
def low(v):
    return lax.optimization_barrier(v.astype(jnp.bfloat16)).astype(jnp.float32)

@jax.custom_vjp
def low_back(v):
    return v

def low_keep(v):
    return (low(v), None)

def low_pass(kept, grad):
    return (grad,)

def back_keep(v):
    return (v, None)

def back_low(kept, grad):
    return (low(grad),)
low.defvjp(low_keep, low_pass)
low_back.defvjp(back_keep, back_low)
HIGHEST = lax.Precision.HIGHEST
EPS_NORM = 1e-06
EPS_UNIT = 1e-06
SIM_SCALE = 16.0
MASKED = -1000000000.0

def both_round(value):
    return low_back(low(value))

def matmul(left, right):
    return jnp.dot(left, right, precision=HIGHEST)

def layer_norm(value, gain, shift):
    row_mean = lax.optimization_barrier(jnp.mean(value, -1, keepdims=True))
    centered = value - row_mean
    row_var = lax.optimization_barrier(jnp.mean(centered * centered, -1, keepdims=True))
    return centered * lax.rsqrt(row_var + EPS_NORM) * gain + shift

def unit_rows(value):
    return value * lax.rsqrt(lax.optimization_barrier(jnp.sum(value * value, -1, keepdims=True)) + EPS_UNIT)

def segments(lengths):
    bounds = NQ + jnp.cumsum(lengths, axis=1, dtype=jnp.int32)
    places = jnp.arange(S, dtype=jnp.int32)
    labels = (places >= NQ).astype(jnp.int32)[None, :] + lax.optimization_barrier(jnp.sum((places[None, None, :] >= bounds[:, :-1, None]).astype(jnp.int32), axis=1))
    return (labels, (bounds - lengths).astype(jnp.int32))

def attend(queries, keys, values, allowed):
    scores = jnp.einsum('gqhe,gkhe->ghqk', queries, keys, precision=HIGHEST) * HEAD_DIM ** (-0.5)
    if allowed is not None:
        scores = jnp.where(allowed[:, None], scores, MASKED)
    attn_probs = low(jax.nn.softmax(low_back(scores), axis=-1))
    return both_round(jnp.einsum('ghqk,gkhe->gqhe', attn_probs, values, precision=HIGHEST))

def layer(hidden, image_rows, lengths, weights):
    self_qkv, self_out, cross_query, cross_kv, cross_out, up_weight, down_weight, norm_gain, norm_bias = weights
    group_size = hidden.shape[0]
    labels, starts = segments(lengths)
    allowed = labels[:, :, None] == labels[:, None, :]
    tokens = hidden.reshape(group_size * S, D)
    shaped = (group_size, S, HEADS, HEAD_DIM)
    heads_in = [both_round(matmul(tokens, self_qkv[index])).reshape(shaped) for index in range(3)]
    mixed_out = attend(heads_in[0], heads_in[1], heads_in[2], allowed).reshape(group_size * S, D)
    normed_one = layer_norm(tokens + low_back(matmul(mixed_out, self_out)), norm_gain[0], norm_bias[0])
    normed_items = normed_one.reshape(group_size, S, D)
    first_query = normed_items[:, :NQ].reshape(group_size * NQ, D)
    cross_heads = both_round(matmul(low(first_query), cross_query)).reshape(group_size, NQ, HEADS, HEAD_DIM)
    feature_rows = image_rows.reshape(group_size * NV, DV)
    vis_shape = (group_size, NV, HEADS, HEAD_DIM)
    cross_keys = both_round(matmul(feature_rows, cross_kv[0])).reshape(vis_shape)
    cross_values = both_round(matmul(feature_rows, cross_kv[1])).reshape(vis_shape)
    cross_mixed = attend(cross_heads, cross_keys, cross_values, None).reshape(group_size * NQ, D)
    normed_query = layer_norm(first_query + low_back(matmul(cross_mixed, cross_out)), norm_gain[1], norm_bias[1])
    normed_two = jnp.concatenate([normed_query.reshape(group_size, NQ, D), normed_items[:, NQ:]], axis=1).reshape(group_size * S, D)
    up_value = low_back(matmul(low(normed_two), up_weight))
    activation = low(jax.nn.gelu(up_value, approximate=False))
    block_value = low(layer_norm(normed_two + low_back(matmul(activation, down_weight)), norm_gain[2], norm_bias[2]))
    return block_value.reshape(group_size, S, D)

def contrast(block_all, lengths, pair_image, vision_proj, text_proj):
    query_out = block_all[:, :NQ].reshape(ITEMS * NQ, D)
    image_all = low_back(matmul(query_out, vision_proj)).reshape(ITEMS, NQ, EMB)
    image_emb = low(unit_rows(lax.optimization_barrier(jnp.mean(image_all, axis=1))))
    labels, starts = segments(lengths)
    picker = (starts[:, :, None] == jnp.arange(S, dtype=jnp.int32)[None, None, :]).astype(jnp.float32)
    cls_rows = jnp.einsum('ics,isd->icd', picker, block_all, precision=HIGHEST).reshape(NTXT, D)
    text_emb = low(unit_rows(low_back(matmul(cls_rows, text_proj))))
    sim_matrix = low_back(matmul(image_emb, text_emb.T) * SIM_SCALE)
    is_pair = pair_image[None, :] == jnp.arange(ITEMS, dtype=jnp.int32)[:, None]
    col_lse = jax.nn.logsumexp(sim_matrix, axis=0)
    col_pos = lax.optimization_barrier(jnp.sum(jnp.where(is_pair, sim_matrix, 0.0), axis=0))
    row_lse = jax.nn.logsumexp(sim_matrix, axis=1)
    row_pos = jax.nn.logsumexp(jnp.where(is_pair, sim_matrix, MASKED), axis=1)
    return 0.5 * jnp.mean(col_lse - col_pos) + 0.5 * jnp.mean(row_lse - row_pos)

def reference(hidden_in, image_feats, caption_lengths, pair_image, out_grad, self_qkv, self_out, cross_query, cross_kv, cross_out, up_weight, down_weight, vision_proj, text_proj, norm_gain, norm_bias):
    weights = tuple((array_in.astype(jnp.float32) for array_in in (self_qkv, self_out, cross_query, cross_kv, cross_out, up_weight, down_weight, vision_proj, text_proj, norm_gain, norm_bias)))
    hidden_f = hidden_in.astype(jnp.float32)
    feats_f = image_feats.astype(jnp.float32)
    cotangent = out_grad.astype(jnp.float32)
    group_size = 32
    groups = ITEMS // group_size
    lengths_grouped = caption_lengths.reshape(groups, group_size, CAPS)

    def objective(hidden_all, feats_all, weight_all):
        layer_weights = weight_all[:7] + weight_all[9:]

        def one_group(packed):
            return layer(packed[0], packed[1], packed[2], layer_weights)
        blocks = lax.map(jax.checkpoint(one_group), (hidden_all.reshape(groups, group_size, S, D), feats_all.reshape(groups, group_size, NV, DV), lengths_grouped))
        block_all = blocks.reshape(ITEMS, S, D)
        loss_value = contrast(block_all, caption_lengths, pair_image, weight_all[7], weight_all[8])
        return (loss_value + jnp.sum(block_all * cotangent), (loss_value, block_all))
    objective_value, pullback, extras = jax.vjp(objective, hidden_f, feats_f, weights, has_aux=True)
    grad_hidden, grad_feats, grad_weights = pullback(jnp.ones_like(objective_value))
    return (extras[0], extras[1].astype(jnp.bfloat16), grad_hidden.astype(jnp.bfloat16), grad_feats.astype(jnp.bfloat16)) + tuple(grad_weights)
```

```python
import jax
import jax.numpy as jnp
from jax import lax
from jax.sharding import PartitionSpec as P

HEAD_DIM = 64
NQ = 32
EPS_NORM = 1e-06
EPS_UNIT = 1e-06
SIM_SCALE = 16.0
MASKED = -1000000000.0
F32 = jnp.float32
BF16 = jnp.bfloat16


def layer_norm(value, gain, shift):
    row_mean = jnp.mean(value, -1, keepdims=True)
    centered = value - row_mean
    row_var = jnp.mean(centered * centered, -1, keepdims=True)
    return centered * lax.rsqrt(row_var + EPS_NORM) * gain + shift


def unit_rows(value):
    return value * lax.rsqrt(jnp.sum(value * value, -1, keepdims=True) + EPS_UNIT)


def gelu_exact(value):
    return jax.nn.gelu(value, approximate=False)


def matmul(left, right):
    return jnp.dot(left, right, preferred_element_type=F32)


def times_rows(left, right):
    return lax.dot_general(left, right, (((1,), (1,)), ((), ())), preferred_element_type=F32)


def times_cols(left, right):
    return lax.dot_general(left, right, (((0,), (0,)), ((), ())), preferred_element_type=F32)


def segments(lengths, seq_len):
    ends = [NQ + lengths[:, 0]]
    for c in range(1, lengths.shape[1]):
        ends.append(ends[-1] + lengths[:, c])
    bounds = jnp.stack(ends, axis=1)
    places = jnp.arange(seq_len, dtype=jnp.int32)
    labels = (places >= NQ).astype(jnp.int32)[None, :] + jnp.sum(
        (places[None, None, :] >= bounds[:, :-1, None]).astype(jnp.int32), axis=1
    )
    return labels, bounds - lengths


def attend_scores(queries_b, keys_b, allowed):
    scores = jnp.einsum("gqhe,gkhe->ghqk", queries_b, keys_b, preferred_element_type=F32) * HEAD_DIM ** (-0.5)
    if allowed is not None:
        scores = jnp.where(allowed[:, None], scores, MASKED)
    return scores


def attend_forward(queries_b, keys_b, values_b, allowed):
    scores = attend_scores(queries_b, keys_b, allowed)
    row_peak = jnp.max(scores, -1, keepdims=True)
    expo = jnp.exp(scores - row_peak)
    row_total = jnp.sum(expo, -1, keepdims=True)
    attn_probs = expo / row_total
    mixed_out = jnp.einsum("ghqk,gkhe->gqhe", attn_probs.astype(BF16), values_b, preferred_element_type=F32)
    return mixed_out.astype(BF16), row_peak + jnp.log(row_total)


def attend_backward(queries_b, keys_b, values_b, allowed, row_lse, grad_mixed):
    scores = attend_scores(queries_b, keys_b, allowed)
    attn_probs = jnp.exp(scores - row_lse)
    grad_probs = jnp.einsum("gqhe,gkhe->ghqk", grad_mixed, values_b, preferred_element_type=F32)
    grad_scores = attn_probs * (grad_probs - jnp.sum(grad_probs * attn_probs, -1, keepdims=True))
    grad_scores_b = grad_scores.astype(BF16)
    scale = HEAD_DIM ** (-0.5)
    grad_queries = jnp.einsum("ghqk,gkhe->gqhe", grad_scores_b, keys_b, preferred_element_type=F32) * scale
    grad_keys = jnp.einsum("ghqk,gqhe->gkhe", grad_scores_b, queries_b, preferred_element_type=F32) * scale
    grad_values = jnp.einsum("ghqk,gqhe->gkhe", attn_probs.astype(BF16), grad_mixed, preferred_element_type=F32)
    return grad_queries.astype(BF16), grad_keys.astype(BF16), grad_values.astype(BF16)


def shards(
    n_dp, n_mp, hidden_in, image_feats, caption_lengths, pair_image, out_grad, self_qkv, self_out, cross_query,
    cross_kv, cross_out, up_weight, down_weight, vision_proj, text_proj, norm_gain, norm_bias,
):
    both = ("mp", "dp")
    me_m = lax.axis_index("mp")
    me_d = lax.axis_index("dp")
    block_items_n, seq_len, width = hidden_in.shape
    items = block_items_n // n_mp
    vis_len, vis_width = image_feats.shape[1:]
    captions = caption_lengths.shape[1]
    tokens_n, query_n, feat_n, text_n = items * seq_len, items * NQ, items * vis_len, items * captions
    lane = self_qkv.shape[2]
    rows, rows_kv = self_qkv.shape[1], cross_kv.shape[1]
    pieces = up_weight.shape[1] // lane
    heads = width // HEAD_DIM
    emb = vision_proj.shape[1]

    def mine(value):
        return lax.dynamic_slice_in_dim(value, me_m * items, items, axis=0)

    hidden = mine(hidden_in)
    feats = mine(image_feats)
    lengths = mine(caption_lengths)
    cotangent = mine(out_grad)

    def cut(value):
        return jnp.moveaxis(value.reshape(value.shape[0], -1, lane), 1, 0).reshape(-1, lane)

    half_emb = emb // n_mp
    vis_half = lax.dynamic_slice_in_dim(vision_proj, me_m * half_emb, half_emb, axis=1)
    txt_half = lax.dynamic_slice_in_dim(text_proj, me_m * half_emb, half_emb, axis=1)
    norms = jnp.concatenate([norm_gain, norm_bias], axis=0).T
    norms = jnp.pad(norms, ((0, 0), (0, lane - 2 * half_emb - norms.shape[1])))
    misc = jnp.concatenate([vis_half, txt_half, norms], axis=1)
    packed = jnp.concatenate(
        [
            self_qkv.reshape(-1, lane), cross_query, self_out.T, misc, cross_kv.reshape(-1, lane), cross_out.T,
            cut(up_weight), cut(down_weight.T),
        ],
        axis=0,
    )
    sizes = [rows] * 6 + [rows_kv] * 2 + [rows] * (1 + 2 * pieces)
    places = [0]
    for size in sizes:
        places.append(places[-1] + size)
    gathered = lax.all_gather(packed, both, axis=0, tiled=False).reshape(n_mp, n_dp, places[-1], lane)

    def part(index):
        return gathered[:, :, places[index] : places[index + 1]].reshape(n_mp, n_dp * sizes[index], lane)

    def wide(value):
        return jnp.moveaxis(value, 0, 1).reshape(value.shape[1], -1)

    w_qkv = [wide(part(j)) for j in range(3)]
    w_query = wide(part(3))
    w_out_t = wide(part(4))
    w_misc = part(5)
    w_kv = [wide(part(6)), wide(part(7))]
    w_cross_out_t = wide(part(8))
    w_up = jnp.stack([part(9 + p) for p in range(pieces)], axis=1)
    w_up = jnp.transpose(w_up, (2, 0, 1, 3)).reshape(width, -1)
    w_down_t = jnp.stack([part(9 + pieces + p) for p in range(pieces)], axis=1)
    w_down_t = jnp.transpose(w_down_t, (2, 0, 1, 3)).reshape(width, -1)
    w_vision = wide(w_misc[:, :, :half_emb])
    w_text = wide(w_misc[:, :, half_emb : 2 * half_emb])
    norm_rows = w_misc[0, :, 2 * half_emb : 2 * half_emb + 6].T.astype(F32)
    gain, shift = norm_rows[:3], norm_rows[3:]

    labels, starts = segments(lengths, seq_len)
    allowed = labels[:, :, None] == labels[:, None, :]
    tokens = hidden.reshape(tokens_n, width)
    shape4 = (items, seq_len, heads, HEAD_DIM)
    q, k, v = (matmul(tokens, w).astype(BF16).reshape(shape4) for w in w_qkv)
    mixed, self_lse = attend_forward(q, k, v, allowed)
    mixed = mixed.reshape(tokens_n, width)
    resid_one = tokens.astype(F32) + times_rows(mixed, w_out_t)
    normed_one = layer_norm(resid_one, gain[0], shift[0])
    normed_items = normed_one.reshape(items, seq_len, width)
    first_query = normed_items[:, :NQ].reshape(query_n, width)
    first_query_b = first_query.astype(BF16)
    cross_q = matmul(first_query_b, w_query).astype(BF16).reshape(items, NQ, heads, HEAD_DIM)
    feat_flat = feats.reshape(feat_n, vis_width)
    shape_vis = (items, vis_len, heads, HEAD_DIM)
    cross_k, cross_v = (matmul(feat_flat, w).astype(BF16).reshape(shape_vis) for w in w_kv)
    cross_mixed, cross_lse = attend_forward(cross_q, cross_k, cross_v, None)
    cross_flat = cross_mixed.reshape(query_n, width)
    resid_two = first_query + times_rows(cross_flat, w_cross_out_t)
    normed_query = layer_norm(resid_two, gain[1], shift[1])
    normed_two = jnp.concatenate(
        [normed_query.reshape(items, NQ, width), normed_items[:, NQ:]], axis=1
    ).reshape(tokens_n, width)
    normed_two_b = normed_two.astype(BF16)
    up_value = matmul(normed_two_b, w_up)
    activation = gelu_exact(up_value).astype(BF16)
    resid_three = normed_two + times_rows(activation, w_down_t)
    block_b = layer_norm(resid_three, gain[2], shift[2]).astype(BF16)
    block_items = block_b.reshape(items, seq_len, width)
    query_out = block_items[:, :NQ].reshape(query_n, width)
    image_raw = jnp.mean(matmul(query_out, w_vision).reshape(items, NQ, emb), axis=1)
    image_b = unit_rows(image_raw).astype(BF16)
    picker = (starts[:, :, None] == jnp.arange(seq_len, dtype=jnp.int32)[None, None, :]).astype(BF16)
    cls_rows = (
        jnp.einsum("ics,isd->icd", picker, block_items, preferred_element_type=F32).astype(BF16).reshape(text_n, width)
    )
    text_raw = matmul(cls_rows, w_text)
    text_b = unit_rows(text_raw).astype(BF16)

    all_pairs = lax.all_gather(pair_image, "dp", axis=0, tiled=True)
    embs = lax.all_gather(jnp.concatenate([image_b, text_b], axis=0), ("dp", "mp"), axis=0, tiled=False)
    all_image = embs[:, :items].reshape(-1, emb)
    all_text = embs[:, items:].reshape(-1, emb)
    image_count, text_count = all_image.shape[0], all_text.shape[0]
    sims = times_rows(all_image, all_text) * SIM_SCALE
    is_pair = all_pairs[None, :] == jnp.arange(image_count, dtype=jnp.int32)[:, None]
    col_peak = jnp.max(sims, axis=0, keepdims=True)
    col_lse = col_peak + jnp.log(jnp.sum(jnp.exp(sims - col_peak), axis=0, keepdims=True))
    row_peak = jnp.max(sims, axis=1, keepdims=True)
    row_expo = jnp.exp(sims - row_peak)
    row_lse = row_peak + jnp.log(jnp.sum(row_expo, axis=1, keepdims=True))
    pair_sims = jnp.where(is_pair, sims, MASKED)
    pos_peak = jnp.max(pair_sims, axis=1, keepdims=True)
    row_pos = pos_peak + jnp.log(jnp.sum(jnp.exp(pair_sims - pos_peak), axis=1, keepdims=True))
    col_pos = jnp.sum(jnp.where(is_pair, sims, 0.0), axis=0, keepdims=True)
    half_image, half_text = 0.5 / image_count, 0.5 / text_count
    contrast_loss = half_text * jnp.sum(col_lse - col_pos) + half_image * jnp.sum(row_lse - row_pos)
    hit = is_pair.astype(F32)
    grad_sims = (
        half_text * (jnp.exp(sims - col_lse) - hit)
        + half_image * (jnp.exp(sims - row_lse) - jnp.where(is_pair, jnp.exp(pair_sims - row_pos), 0.0))
    ).astype(BF16)
    first_image = (me_d * n_mp + me_m) * items
    own_rows = lax.dynamic_slice_in_dim(grad_sims, first_image, items, axis=0)
    own_cols = lax.dynamic_slice_in_dim(grad_sims, first_image * captions, text_n, axis=1)
    grad_image_unit = matmul(own_rows, all_text) * SIM_SCALE
    grad_text_unit = times_cols(own_cols, all_image) * SIM_SCALE
    grad_image_raw = jax.vjp(unit_rows, image_raw)[1](grad_image_unit)[0]
    grad_image_all = (
        jnp.broadcast_to((grad_image_raw / NQ)[:, None, :], (items, NQ, emb)).reshape(query_n, emb).astype(BF16)
    )
    grad_vision = times_cols(query_out, grad_image_all)
    grad_text_raw = jax.vjp(unit_rows, text_raw)[1](grad_text_unit)[0].astype(BF16)
    grad_text = times_cols(cls_rows, grad_text_raw)
    query_grad = times_rows(grad_image_all, w_vision).reshape(items, NQ, width)
    spread_text = jnp.einsum(
        "ics,ice->ise", picker, grad_text_raw.reshape(items, captions, emb), preferred_element_type=F32
    ).astype(BF16)
    spread = times_rows(spread_text.reshape(tokens_n, emb), w_text).reshape(items, seq_len, width)
    query_pad = jnp.concatenate([query_grad, jnp.zeros((items, seq_len - NQ, width), F32)], axis=1)
    grad_items = (cotangent.astype(F32) + spread + query_pad).reshape(tokens_n, width)
    grad_resid_three, grad_gain_three, grad_shift_three = jax.vjp(layer_norm, resid_three, gain[2], shift[2])[1](grad_items)
    grad_branch_three = grad_resid_three.astype(BF16)
    grad_down_t = times_cols(grad_branch_three, activation)
    grad_activation = matmul(grad_branch_three, w_down_t)
    grad_up_value = jax.vjp(gelu_exact, up_value)[1](grad_activation)[0].astype(BF16)
    grad_up = times_cols(normed_two_b, grad_up_value)
    grad_normed_two = grad_resid_three + times_rows(grad_up_value, w_up)
    grad_two_items = grad_normed_two.reshape(items, seq_len, width)
    grad_two_query = grad_two_items[:, :NQ].reshape(query_n, width)
    grad_resid_two, grad_gain_two, grad_shift_two = jax.vjp(layer_norm, resid_two, gain[1], shift[1])[1](grad_two_query)
    grad_branch_two = grad_resid_two.astype(BF16)
    grad_cross_out_t = times_cols(grad_branch_two, cross_flat)
    grad_cross_mixed = matmul(grad_branch_two, w_cross_out_t).astype(BF16).reshape(items, NQ, heads, HEAD_DIM)
    grad_cross_q, grad_cross_k, grad_cross_v = attend_backward(
        cross_q, cross_k, cross_v, None, cross_lse, grad_cross_mixed
    )
    grad_cross_q = grad_cross_q.reshape(query_n, width)
    grad_cross_query = times_cols(first_query_b, grad_cross_q)
    grad_first_query = grad_resid_two + times_rows(grad_cross_q, w_query)
    grad_cross_k = grad_cross_k.reshape(feat_n, width)
    grad_cross_v = grad_cross_v.reshape(feat_n, width)
    grad_feats = (
        (times_rows(grad_cross_k, w_kv[0]) + times_rows(grad_cross_v, w_kv[1])).astype(BF16).reshape(feats.shape)
    )
    grad_feats_far = lax.ppermute(grad_feats, "mp", [(i, i ^ 1) for i in range(n_mp)])
    grad_kv = [times_cols(feat_flat, grad_cross_k), times_cols(feat_flat, grad_cross_v)]
    grad_one = jnp.concatenate(
        [grad_first_query.reshape(items, NQ, width), grad_two_items[:, NQ:]], axis=1
    ).reshape(tokens_n, width)
    grad_resid_one, grad_gain_one, grad_shift_one = jax.vjp(layer_norm, resid_one, gain[0], shift[0])[1](grad_one)
    grad_branch_one = grad_resid_one.astype(BF16)
    grad_self_out_t = times_cols(grad_branch_one, mixed)
    grad_mixed = matmul(grad_branch_one, w_out_t).astype(BF16).reshape(shape4)
    grad_heads = attend_backward(q, k, v, allowed, self_lse, grad_mixed)
    grad_heads = [g.reshape(tokens_n, width) for g in grad_heads]
    grad_qkv = [times_cols(tokens, g) for g in grad_heads]
    grad_tokens = grad_resid_one
    for j in range(3):
        grad_tokens = grad_tokens + times_rows(grad_heads[j], w_qkv[j])
    grad_hidden = grad_tokens.astype(BF16).reshape(hidden.shape)

    def narrow(value, size):
        return jnp.transpose(value.reshape(n_dp, size, n_mp, -1, lane), (2, 0, 3, 1, 4)).reshape(n_mp, n_dp, -1, lane)

    def halves(value):
        return jnp.transpose(value.reshape(n_dp, rows, n_mp, half_emb), (2, 0, 1, 3))

    norm_grads = jnp.stack(
        [grad_gain_one, grad_gain_two, grad_gain_three, grad_shift_one, grad_shift_two, grad_shift_three], axis=1
    ).reshape(1, n_dp, rows, 6)
    norm_grads = jnp.concatenate([norm_grads] + [jnp.zeros_like(norm_grads)] * (n_mp - 1), axis=0)
    misc_grad = jnp.concatenate(
        [
            halves(grad_vision), halves(grad_text), norm_grads,
            jnp.zeros((n_mp, n_dp, rows, lane - 2 * half_emb - 6), F32),
        ],
        axis=3,
    )
    packed_grad = jnp.concatenate(
        [
            value.astype(BF16)
            for value in [narrow(g, rows) for g in grad_qkv]
            + [narrow(grad_cross_query, rows), narrow(grad_self_out_t, rows), misc_grad]
            + [narrow(g, rows_kv) for g in grad_kv]
            + [narrow(grad_cross_out_t, rows), narrow(grad_up, rows), narrow(grad_down_t, rows)]
        ],
        axis=2,
    ).reshape(n_mp * n_dp, places[-1], lane)
    summed = lax.psum_scatter(packed_grad, both, scatter_dimension=0, tiled=False).astype(F32)

    def share(first, last):
        return summed[places[first] : places[last]]

    def uncut(value):
        return jnp.moveaxis(value.reshape(pieces, rows, lane), 0, 1).reshape(rows, pieces * lane)

    misc_share = share(5, 6).astype(BF16)
    misc_far = lax.ppermute(misc_share, "mp", [(i, i ^ 1) for i in range(n_mp)])
    low = jnp.where(me_m == 0, misc_share, misc_far).astype(F32)
    high = jnp.where(me_m == 0, misc_far, misc_share).astype(F32)
    norm_share = low[:, 2 * half_emb : 2 * half_emb + 6].T

    def whole(own, far):
        low_part = jnp.where(me_m == 0, own, far)
        high_part = jnp.where(me_m == 0, far, own)
        return jnp.concatenate([low_part, high_part], axis=0)

    def exchanged(value):
        return whole(value, lax.ppermute(value, "mp", [(i, i ^ 1) for i in range(n_mp)]))

    return (
        contrast_loss,
        exchanged(block_items),
        exchanged(grad_hidden),
        whole(grad_feats, grad_feats_far),
        share(0, 3).reshape(3, rows, lane),
        share(4, 5).T,
        share(3, 4),
        share(6, 8).reshape(2, rows_kv, lane),
        share(8, 9).T,
        uncut(share(9, 9 + pieces)),
        uncut(share(9 + pieces, 9 + 2 * pieces)).T,
        jnp.concatenate([low[:, :half_emb], high[:, :half_emb]], axis=1),
        jnp.concatenate([low[:, half_emb : 2 * half_emb], high[:, half_emb : 2 * half_emb]], axis=1),
        norm_share[:3],
        norm_share[3:],
    )


def solution(mesh):
    n_dp, n_mp = mesh.shape["dp"], mesh.shape["mp"]

    def body(*args):
        return shards(n_dp, n_mp, *args)

    return jax.shard_map(
        body,
        mesh=mesh,
        in_specs=(
            P("dp", None, None),
            P("dp", None, None),
            P("dp", None),
            P("dp"),
            P("dp", None, None),
            P(None, "dp", "mp"),
            P("mp", "dp"),
            P("dp", "mp"),
            P(None, "dp", "mp"),
            P("mp", "dp"),
            P("dp", "mp"),
            P("mp", "dp"),
            P("dp", None),
            P("dp", None),
            P(None, "dp"),
            P(None, "dp"),
        ),
        out_specs=(
            P(),
            P("dp", None, None),
            P("dp", None, None),
            P("dp", None, None),
            P(None, "dp", "mp"),
            P("mp", "dp"),
            P("dp", "mp"),
            P(None, "dp", "mp"),
            P("mp", "dp"),
            P("dp", "mp"),
            P("mp", "dp"),
            P("dp", None),
            P("dp", None),
            P(None, "dp"),
            P(None, "dp"),
        ),
        check_vma=False,
    )
```

```python
import functools

import jax
import jax.numpy as jnp
from jax import lax
from jax.experimental import pallas as pl
from jax.experimental.pallas import tpu as pltpu
from jax.sharding import PartitionSpec as P

HEAD_DIM = 64
NQ = 32
EPS_NORM = 1e-06
EPS_UNIT = 1e-06
SIM_SCALE = 16.0
MASKED = -1000000000.0
F32 = jnp.float32
BF16 = jnp.bfloat16


def dot(left, right):
    return jnp.dot(left, right, preferred_element_type=F32)


def dot_nt(left, right):
    return lax.dot_general(left, right, (((1,), (1,)), ((), ())), preferred_element_type=F32)


def dot_tn(left, right):
    return lax.dot_general(left, right, (((0,), (0,)), ((), ())), preferred_element_type=F32)


def iota(shape, dim):
    return lax.broadcasted_iota(jnp.int32, shape, dim)


def norm_forward(value, gain, shift):
    mean = jnp.mean(value, -1, keepdims=True)
    centered = value - mean
    scale = lax.rsqrt(jnp.mean(centered * centered, -1, keepdims=True) + EPS_NORM)
    return centered * scale * gain + shift


def norm_backward(value, grad, gain):
    mean = jnp.mean(value, -1, keepdims=True)
    centered = value - mean
    scale = lax.rsqrt(jnp.mean(centered * centered, -1, keepdims=True) + EPS_NORM)
    unit = centered * scale
    inner = grad * gain
    back = scale * (inner - jnp.mean(inner, -1, keepdims=True) - unit * jnp.mean(inner * unit, -1, keepdims=True))
    return back, jnp.sum(grad * unit, 0, keepdims=True), jnp.sum(grad, 0, keepdims=True)


def low_lanes(rows):
    return iota((rows, 2 * HEAD_DIM), 1) < HEAD_DIM


def pair_rows(value):
    low = low_lanes(value.shape[0])
    value = value.astype(F32)
    zero = jnp.zeros_like(value)
    return jnp.concatenate([jnp.where(low, value, zero), jnp.where(low, zero, value)], axis=0).astype(BF16)


def merge_rows(value):
    half = value.shape[0] // 2
    return jnp.where(low_lanes(half), value[:half], value[half:])


def probabilities(queries, keys, keep):
    scores = dot_nt(queries, keys) * HEAD_DIM ** (-0.5)
    scores = jnp.where(keep, scores, MASKED)
    expo = jnp.exp(scores - jnp.max(scores, -1, keepdims=True))
    return expo / jnp.sum(expo, -1, keepdims=True)


def attention_back(queries, keys, values, grads, keep):
    probs = probabilities(queries, keys, keep)
    grad_probs = dot_nt(grads, values)
    grad_scores = (probs * (grad_probs - jnp.sum(grad_probs * probs, -1, keepdims=True))).astype(BF16)
    scale = HEAD_DIM ** (-0.5)
    grad_q = merge_rows(dot(grad_scores, keys)) * scale
    grad_k = dot_tn(grad_scores, queries) * scale
    grad_v = dot_tn(probs.astype(BF16), grads)
    return grad_q.astype(BF16), grad_k.astype(BF16), grad_v.astype(BF16)


def same_segment(lens_ref, item, rows, keys):
    first = NQ + lens_ref[item, 0]
    second = first + lens_ref[item, 1]

    def label(place):
        return (
            (place >= NQ).astype(jnp.int32) + (place >= first).astype(jnp.int32) + (place >= second).astype(jnp.int32)
        )

    return label(iota((rows, keys), 0) & (keys - 1)) == label(iota((rows, keys), 1))


def aligned(index, step):
    return pl.ds(pl.multiple_of(index * step, step), step)


def fetch(weights, part, chunk_rows, target, sems, first):
    lane = weights.shape[3]
    copies = []
    for m in range(weights.shape[0]):
        copies.append(
            pltpu.make_async_copy(
                weights.at[m, :, pl.ds(part * chunk_rows, chunk_rows), :],
                target.at[:, :, pl.ds(m * lane, lane)],
                sems.at[first + m],
            )
        )
        copies[-1].start()
    return copies


def fetch_tile(weights, part, chunk_rows, target, lane_at, m, sem):
    lane = weights.shape[3]
    copy = pltpu.make_async_copy(
        weights.at[m, :, pl.ds(part * chunk_rows, chunk_rows), :], target.at[:, :, pl.ds(lane_at, lane)], sem
    )
    copy.start()
    return copy


def flat(ref_value):
    return ref_value.reshape(-1, ref_value.shape[-1])


def store_halves(out_ref, row_at, chunk_rows, stored, value, m_of, d_of):
    n_mp, n_chunk, _, lane = out_ref.shape
    if stored != chunk_rows:
        value = jnp.concatenate([value, jnp.zeros((stored - chunk_rows, value.shape[1]), value.dtype)], axis=0)
    for m in range(value.shape[1] // lane):
        for d in range(n_chunk):
            out_ref[m_of(m), d_of(d), pl.ds(row_at, stored), :] = value[
                d * chunk_rows : d * chunk_rows + stored, m * lane : (m + 1) * lane
            ].astype(BF16)


def self_forward(lens_ref, hid_ref, norm_ref, w_ref, qkv_ref, mixed_ref, resid_ref, normed_ref, fq_ref, cq_ref, wbuf, sems):
    items = lens_ref.shape[0]
    seq = hid_ref.shape[0] // items
    width = hid_ref.shape[1]
    rc = wbuf.shape[2]
    copies = [fetch(w_ref, p, rc, wbuf.at[p], sems, p * w_ref.shape[0]) for p in range(5)]
    x = hid_ref[...]
    for j in range(3):
        for c in copies[j]:
            c.wait()
        qkv_ref[j] = dot(x, flat(wbuf[j])).astype(BF16)

    def one(item, carry):
        rows = aligned(item, seq)
        keep = same_segment(lens_ref, item, 2 * seq, seq)
        for p in range(width // 128):
            lanes = pl.ds(p * 128, 128)
            probs = probabilities(pair_rows(qkv_ref[0, rows, lanes]), qkv_ref[1, rows, lanes], keep)
            mixed_ref[rows, lanes] = merge_rows(dot(probs.astype(BF16), qkv_ref[2, rows, lanes])).astype(BF16)
        return carry

    lax.fori_loop(0, items, one, 0)
    for p in (3, 4):
        for c in copies[p]:
            c.wait()
    resid = x.astype(F32) + dot_nt(mixed_ref[...], flat(wbuf[4]))
    resid_ref[...] = resid
    normed = norm_forward(resid, norm_ref[0:1], norm_ref[3:4])
    normed_ref[...] = normed
    query = jnp.concatenate([normed[i * seq : i * seq + NQ] for i in range(items)], axis=0).astype(BF16)
    fq_ref[...] = query
    cq_ref[...] = dot(query, flat(wbuf[3])).astype(BF16)


def cross_forward(
    vis_len, normed_ref, cq_ref, feat_ref, kvw_ref, norm_ref, w_ref, kv_ref, mixed_ref, resid_ref, two_ref, wbuf, sems
):
    items = cq_ref.shape[0] // NQ
    seq = normed_ref.shape[0] // items
    width = cq_ref.shape[1]
    vis_pad = feat_ref.shape[0] // items
    copies = fetch(w_ref, 5, wbuf.shape[1], wbuf, sems, 0)
    step = 256
    for j in range(2):

        def project(n, carry, j=j):
            lanes = aligned(n, step)
            kv_ref[j, :, lanes] = dot(feat_ref[...], kvw_ref[j, :, lanes]).astype(BF16)
            return carry

        lax.fori_loop(0, width // step, project, 0)

    def one(item, carry):
        rows, keys = aligned(item, NQ), aligned(item, vis_pad)
        keep = iota((2 * NQ, vis_pad), 1) < vis_len
        for p in range(width // 128):
            lanes = pl.ds(p * 128, 128)
            probs = probabilities(pair_rows(cq_ref[rows, lanes]), kv_ref[0, keys, lanes], keep)
            mixed_ref[rows, lanes] = merge_rows(dot(probs.astype(BF16), kv_ref[1, keys, lanes])).astype(BF16)
        return carry

    lax.fori_loop(0, items, one, 0)
    for c in copies:
        c.wait()
    first = jnp.concatenate([normed_ref[i * seq : i * seq + NQ] for i in range(items)], axis=0)
    resid = first + dot_nt(mixed_ref[...], flat(wbuf[...]))
    resid_ref[...] = resid
    normed = norm_forward(resid, norm_ref[1:2], norm_ref[4:5])
    for i in range(items):
        two_ref[i * seq : i * seq + NQ] = normed[i * NQ : (i + 1) * NQ]
        two_ref[i * seq + NQ : (i + 1) * seq] = normed_ref[i * seq + NQ : (i + 1) * seq]


def picker_of(lens_ref, rows, seq):
    items, captions = lens_ref.shape
    shape = (rows, items * seq)
    row = iota(shape, 0)
    target = jnp.full(shape, -1, jnp.int32)
    for i in range(items):
        start = i * seq + NQ
        for c in range(captions):
            target = jnp.where(row == i * captions + c, start, target)
            start = start + lens_ref[i, c]
    return (target == iota(shape, 1)).astype(F32).astype(BF16)


def unit_forward(value):
    return value * lax.rsqrt(jnp.sum(value * value, -1, keepdims=True) + EPS_UNIT)


def unit_backward(value, grad):
    scale = lax.rsqrt(jnp.sum(value * value, -1, keepdims=True) + EPS_UNIT)
    return grad * scale - value * (scale * scale * scale * jnp.sum(grad * value, -1, keepdims=True))


def ffn_fetch(w_ref, up_buf, down_buf, sems):
    n_mp, lane = w_ref.shape[0], w_ref.shape[3]
    tiles, _, rc, tile = up_buf.shape
    per = tile // lane
    pieces = tiles * per // n_mp
    ups, downs = [[] for _ in range(tiles)], [[] for _ in range(tiles)]
    for t in range(tiles):
        for s in range(per):
            piece = t * per + s
            m, p = piece // pieces, piece % pieces
            ups[t].append(fetch_tile(w_ref, 6 + p, rc, up_buf.at[t], s * lane, m, sems.at[2 * piece]))
            downs[t].append(fetch_tile(w_ref, 6 + pieces + p, rc, down_buf.at[t], s * lane, m, sems.at[2 * piece + 1]))
    return ups, downs


def misc_fetch(w_ref, part, misc_buf, sems):
    rc = misc_buf.shape[2]
    copies = []
    for m in range(w_ref.shape[0]):
        copies.append(
            pltpu.make_async_copy(w_ref.at[m, :, pl.ds(part * rc, rc), :], misc_buf.at[m], sems.at[m])
        )
        copies[-1].start()
    return copies


def ffn_forward(
    lens_ref, two_ref, norm_ref, w_ref, up_ref, act_ref, resid_ref, block_ref, cls_ref, iraw_ref, traw_ref, emb_ref,
    up_buf, down_buf, misc_buf, sems, msems,
):
    items, captions = lens_ref.shape
    seq = two_ref.shape[0] // items
    tiles = up_buf.shape[0]
    n_mp, lane = w_ref.shape[0], w_ref.shape[3]
    ups, downs = ffn_fetch(w_ref, up_buf, down_buf, sems)
    miscs = misc_fetch(w_ref, 6 + 2 * (tiles * (up_buf.shape[3] // lane) // n_mp), misc_buf, msems)
    two = two_ref[...]
    two_b = two.astype(BF16)
    resid = two
    for t in range(tiles):
        for c in ups[t]:
            c.wait()
        up = dot(two_b, flat(up_buf[t]))
        up_ref[t] = up
        act = (0.5 * up * (1.0 + lax.erf(up * (0.5**0.5)))).astype(BF16)
        act_ref[t] = act
        for c in downs[t]:
            c.wait()
        resid = resid + dot_nt(act, flat(down_buf[t]))
    resid_ref[...] = resid
    block = norm_forward(resid, norm_ref[2:3], norm_ref[5:6]).astype(BF16)
    block_ref[...] = block
    rows = iraw_ref.shape[0]
    cls = dot(picker_of(lens_ref, rows, seq), block).astype(BF16)
    cls_ref[...] = cls
    query = jnp.concatenate([block[i * seq : i * seq + NQ] for i in range(items)], axis=0)
    for c in miscs:
        c.wait()
    half = iraw_ref.shape[1] // n_mp
    row = iota((rows, half), 0)
    for m in range(n_mp):
        misc = flat(misc_buf[m])
        image = dot(query, misc[:, :half])
        raw = jnp.zeros((rows, half), F32)
        for i in range(items):
            raw = jnp.where(row == i, jnp.sum(image[i * NQ : (i + 1) * NQ], 0, keepdims=True) * (1.0 / NQ), raw)
        iraw_ref[:, m * half : (m + 1) * half] = raw
        traw_ref[:, m * half : (m + 1) * half] = dot(cls, misc[:, half : 2 * half])
    image_b = unit_forward(iraw_ref[...]).astype(BF16)
    text_b = unit_forward(traw_ref[...]).astype(BF16)
    r, c = iota((rows, rows), 0), iota((rows, rows), 1)
    put_image = ((r == c) & (r < items)).astype(F32).astype(BF16)
    put_text = ((r == c + items) & (c < items * captions)).astype(F32).astype(BF16)
    emb_ref[...] = (dot(put_image, image_b) + dot(put_text, text_b)).astype(BF16)


def device_of(place, shift, me):
    place = place >> shift
    relative = ((place >> 3) & 1) + 2 * (place >> 4) + 4 * ((place >> 2) & 1) + 8 * (place & 3)
    return relative ^ me


def contrast(items, captions, me_ref, emb_ref, pair_ref, iraw_ref, traw_ref, loss_ref, gi_ref, gt_ref):
    me = me_ref[0]
    rows = iraw_ref.shape[0]
    n_dev = emb_ref.shape[0] // rows
    shift = rows.bit_length() - 1
    images, texts = n_dev * items, n_dev * captions * items
    emb = emb_ref[...]
    r, c = iota((images, n_dev * rows), 0), iota((images, n_dev * rows), 1)
    slot = c & (rows - 1)
    pick = ((device_of(c, shift, me) * items + slot == r) & (slot < items)).astype(F32).astype(BF16)
    image = dot(pick, emb).astype(BF16)
    r, c = iota((texts, n_dev * rows), 0), iota((texts, n_dev * rows), 1)
    slot = (c & (rows - 1)) - items
    pick = ((device_of(c, shift, me) * (items * captions) + slot == r) & (slot >= 0)).astype(F32).astype(BF16)
    text = dot(pick, emb).astype(BF16)
    sims = dot_nt(image, text) * SIM_SCALE
    is_pair = pair_ref[...] == iota((images, texts), 0)
    col_peak = jnp.max(sims, 0, keepdims=True)
    col_lse = col_peak + jnp.log(jnp.sum(jnp.exp(sims - col_peak), 0, keepdims=True))
    row_peak = jnp.max(sims, 1, keepdims=True)
    row_lse = row_peak + jnp.log(jnp.sum(jnp.exp(sims - row_peak), 1, keepdims=True))
    pair_sims = jnp.where(is_pair, sims, MASKED)
    pos_peak = jnp.max(pair_sims, 1, keepdims=True)
    row_pos = pos_peak + jnp.log(jnp.sum(jnp.exp(pair_sims - pos_peak), 1, keepdims=True))
    col_pos = jnp.sum(jnp.where(is_pair, sims, 0.0), 0, keepdims=True)
    half_image, half_text = 0.5 / images, 0.5 / texts
    loss_ref[...] = half_text * jnp.sum(col_lse - col_pos, axis=1, keepdims=True) + half_image * jnp.sum(
        row_lse - row_pos, axis=0, keepdims=True
    )
    hit = jnp.where(is_pair, 1.0, 0.0)
    grad = (
        half_text * (jnp.exp(sims - col_lse) - hit)
        + half_image * (jnp.exp(sims - row_lse) - jnp.exp(pair_sims - row_pos))
    ).astype(BF16)
    r, c = iota((rows, images), 0), iota((rows, images), 1)
    own = ((c == me * items + r) & (r < items)).astype(F32).astype(BF16)
    grad_image = dot(dot(own, grad).astype(BF16), text) * SIM_SCALE
    r, c = iota((rows, texts), 0), iota((rows, texts), 1)
    own = ((c == me * (items * captions) + r) & (r < items * captions)).astype(F32).astype(BF16)
    grad_text = dot(dot_nt(own, grad).astype(BF16), image) * SIM_SCALE
    gi_ref[...] = (unit_backward(iraw_ref[...], grad_image) * (1.0 / NQ)).astype(BF16)
    gt_ref[...] = unit_backward(traw_ref[...], grad_text).astype(BF16)


def ffn_backward(
    lens_ref, me_ref, gi_ref, gt_ref, block_ref, cls_ref, og_ref, two_ref, resid_ref, up_ref, act_ref, norm_ref, w_ref,
    gtwo_ref, ng_ref, gw_ref, up_buf, down_buf, misc_buf, sems, msems,
):
    items = lens_ref.shape[0]
    seq = two_ref.shape[0] // items
    tokens = two_ref.shape[0]
    tiles, nc, rc, tile = up_buf.shape
    n_mp, lane = w_ref.shape[0], w_ref.shape[3]
    per = tile // lane
    pieces = tiles * per // n_mp
    miscs = misc_fetch(w_ref, 6 + 2 * pieces, misc_buf, msems)
    ups, downs = ffn_fetch(w_ref, up_buf, down_buf, sems)
    rows, emb = gi_ref.shape
    half = emb // n_mp
    gi, gt = gi_ref[...], gt_ref[...]
    r, c = iota((tokens, rows), 0), iota((tokens, rows), 1)
    spread = (((r // seq) == c) & ((r & (seq - 1)) < NQ)).astype(F32).astype(BF16)
    gi_rows = dot(spread, gi).astype(BF16)
    gt_rows = dot_tn(picker_of(lens_ref, rows, seq), gt).astype(BF16)
    for c in miscs:
        c.wait()
    grad = og_ref[...].astype(F32)
    block = block_ref[...]
    cls = cls_ref[...]
    zero = jnp.zeros((rc * nc, lane - 2 * half), F32)
    for m in range(n_mp):
        misc = flat(misc_buf[m])
        lanes = slice(m * half, (m + 1) * half)
        grad = grad + dot_nt(gi_rows[:, lanes], misc[:, :half]) + dot_nt(gt_rows[:, lanes], misc[:, half : 2 * half])
        share = jnp.concatenate([dot_tn(block, gi_rows[:, lanes]), dot_tn(cls, gt[:, lanes]), zero], axis=1)
        store_halves(gw_ref, 2 * pieces * rc, rc, rc, share, lambda _, m=m: m ^ me_ref[1], lambda d: d ^ me_ref[2])
    back, gain_grad, shift_grad = norm_backward(resid_ref[...], grad, norm_ref[2:3])
    ng_ref[...] = jnp.concatenate([gain_grad, shift_grad], axis=0)
    branch = back.astype(BF16)
    two_b = two_ref[...].astype(BF16)
    total = back
    for t in range(tiles):
        for c in downs[t] + ups[t]:
            c.wait()
        up = up_ref[t]
        slope = 0.5 * (1.0 + lax.erf(up * (0.5**0.5))) + up * jnp.exp(-0.5 * up * up) * 0.3989422804014327
        grad_up = (dot(branch, flat(down_buf[t])) * slope).astype(BF16)
        m, p = (t * per) // pieces, (t * per) % pieces
        for s in range(per):
            lanes = slice(s * lane, (s + 1) * lane)
            for base, left, right in ((0, two_b, grad_up), (pieces, branch, act_ref[t])):
                store_halves(
                    gw_ref, (base + p + s) * rc, rc, rc, dot_tn(left, right[:, lanes]),
                    lambda _, m=m: m ^ me_ref[1], lambda d: d ^ me_ref[2],
                )
        total = total + dot_nt(grad_up, flat(up_buf[t]))
    gtwo_ref[...] = total


def cross_backward(
    vis_len, rc, me_ref, gtwo_ref, resid_ref, mixed_ref, cq_ref, fq_ref, kv_ref, kvw_ref, norm_ref, w_ref,
    gone_ref, ng_ref, gkv_ref, gf_ref, gw_ref, wbuf, gq_buf, sems,
):
    items = cq_ref.shape[0] // NQ
    seq = gtwo_ref.shape[0] // items
    width = cq_ref.shape[1]
    vis_pad = kv_ref.shape[1] // items
    wrc = wbuf.shape[2]
    n_mp = w_ref.shape[0]
    copies = [fetch(w_ref, p, wrc, wbuf.at[i], sems, i * n_mp) for i, p in enumerate((5, 3))]
    xor_m, xor_d = (lambda m: m ^ me_ref[1]), (lambda d: d ^ me_ref[2])
    grad = jnp.concatenate([gtwo_ref[i * seq : i * seq + NQ] for i in range(items)], axis=0)
    back, gain_grad, shift_grad = norm_backward(resid_ref[...], grad, norm_ref[1:2])
    ng_ref[...] = jnp.concatenate([gain_grad, shift_grad], axis=0)
    branch = back.astype(BF16)
    for c in copies[0]:
        c.wait()
    grad_mixed = dot(branch, flat(wbuf[0])).astype(BF16)
    gq_buf[...] = grad_mixed

    def one(item, carry):
        rows, keys = aligned(item, NQ), aligned(item, vis_pad)
        keep = iota((2 * NQ, vis_pad), 1) < vis_len
        for p in range(width // 128):
            lanes = pl.ds(p * 128, 128)
            grad_q, grad_k, grad_v = attention_back(
                pair_rows(cq_ref[rows, lanes]), kv_ref[0, keys, lanes], kv_ref[1, keys, lanes],
                pair_rows(gq_buf[rows, lanes]), keep,
            )
            gq_buf[rows, lanes] = grad_q
            gkv_ref[0, keys, lanes] = grad_k
            gkv_ref[1, keys, lanes] = grad_v
        return carry

    lax.fori_loop(0, items, one, 0)
    step = 128

    def feats(n, carry):
        lanes = aligned(n, step)
        gf_ref[:, lanes] = (
            dot_nt(gkv_ref[0], kvw_ref[0, lanes, :]) + dot_nt(gkv_ref[1], kvw_ref[1, lanes, :])
        ).astype(BF16)
        return carry

    lax.fori_loop(0, gf_ref.shape[1] // step, feats, 0)
    store_halves(gw_ref, 0, rc, rc, dot_tn(branch, mixed_ref[...]), xor_m, xor_d)
    store_halves(gw_ref, rc, rc, rc, dot_tn(fq_ref[...], gq_buf[...]), xor_m, xor_d)
    for c in copies[1]:
        c.wait()
    first = back + dot_nt(gq_buf[...], flat(wbuf[1]))
    for i in range(items):
        gone_ref[i * seq : i * seq + NQ] = first[i * NQ : (i + 1) * NQ]
        gone_ref[i * seq + NQ : (i + 1) * seq] = gtwo_ref[i * seq + NQ : (i + 1) * seq]


def kv_backward(rk, stored, me_ref, feat_t_ref, gkv_ref, gw_ref):
    for j in range(2):
        store_halves(
            gw_ref, j * stored, rk, stored, dot(feat_t_ref[...], gkv_ref[j]),
            lambda m: m ^ me_ref[1], lambda d: d ^ me_ref[2],
        )


def self_backward(
    rc, lens_ref, me_ref, gone_ref, resid_ref, hid_ref, mixed_ref, qkv_ref, norm_ref, ngb_ref, ngc_ref, w_ref,
    gh_ref, gw_ref, wbuf, gm_buf, gqkv_buf, sems,
):
    items = lens_ref.shape[0]
    seq = hid_ref.shape[0] // items
    width = hid_ref.shape[1]
    n_mp = w_ref.shape[0]
    copies = [fetch(w_ref, p, wbuf.shape[2], wbuf.at[i], sems, i * n_mp) for i, p in enumerate((4, 0, 1, 2))]
    xor_m, xor_d = (lambda m: m ^ me_ref[1]), (lambda d: d ^ me_ref[2])
    back, gain_grad, shift_grad = norm_backward(resid_ref[...], gone_ref[...], norm_ref[0:1])
    branch = back.astype(BF16)
    for c in copies[0]:
        c.wait()
    gm_buf[...] = dot(branch, flat(wbuf[0])).astype(BF16)

    def one(item, carry):
        rows = aligned(item, seq)
        keep = same_segment(lens_ref, item, 2 * seq, seq)
        for p in range(width // 128):
            lanes = pl.ds(p * 128, 128)
            grads = attention_back(
                pair_rows(qkv_ref[0, rows, lanes]), qkv_ref[1, rows, lanes], qkv_ref[2, rows, lanes],
                pair_rows(gm_buf[rows, lanes]), keep,
            )
            for j in range(3):
                gqkv_buf[j, rows, lanes] = grads[j]
        return carry

    lax.fori_loop(0, items, one, 0)
    x = hid_ref[...]
    for j in range(3):
        store_halves(gw_ref, j * rc, rc, rc, dot_tn(x, gqkv_buf[j]), xor_m, xor_d)
    store_halves(gw_ref, 3 * rc, rc, rc, dot_tn(branch, mixed_ref[...]), xor_m, xor_d)
    norms = jnp.concatenate(
        [gain_grad, ngb_ref[0:1], ngc_ref[0:1], shift_grad, ngb_ref[1:2], ngc_ref[1:2], jnp.zeros((122, width), F32)],
        axis=0,
    ).T
    lane = gw_ref.shape[3]
    norms = jnp.concatenate([norms, jnp.zeros((width, lane - 128), F32)], axis=1)
    for m in range(gw_ref.shape[0]):
        store_halves(gw_ref, 4 * rc, rc, rc, norms if m == 0 else jnp.zeros_like(norms), lambda _, m=m: m ^ me_ref[1], xor_d)
    total = back
    for j in range(3):
        for c in copies[j + 1]:
            c.wait()
        total = total + dot_nt(gqkv_buf[j], flat(wbuf[j + 1]))
    gh_ref[...] = total.astype(BF16)


def run(body, outs, scratch, *ins):
    spaces = {"v": pltpu.VMEM, "s": pltpu.SMEM, "a": pl.ANY}
    return pl.pallas_call(
        body,
        out_shape=[jax.ShapeDtypeStruct(shape, dtype) for shape, dtype in outs],
        in_specs=[pl.BlockSpec(memory_space=spaces[kind]) for kind, _ in ins],
        out_specs=[pl.BlockSpec(memory_space=pltpu.VMEM) for _ in outs],
        scratch_shapes=scratch,
        compiler_params=pltpu.CompilerParams(vmem_limit_bytes=60 * 1024 * 1024),
    )(*[value for _, value in ins])


def contrast_plain(all_image, all_text, all_pairs, image_raw, text_raw, first_image):
    items, text_n = image_raw.shape[0], text_raw.shape[0]
    captions = text_n // items
    image_count, text_count = all_image.shape[0], all_text.shape[0]
    sims = dot_nt(all_image, all_text) * SIM_SCALE
    is_pair = all_pairs == jnp.arange(image_count, dtype=jnp.int32)[:, None]
    col_peak = jnp.max(sims, axis=0, keepdims=True)
    col_lse = col_peak + jnp.log(jnp.sum(jnp.exp(sims - col_peak), axis=0, keepdims=True))
    row_peak = jnp.max(sims, axis=1, keepdims=True)
    row_lse = row_peak + jnp.log(jnp.sum(jnp.exp(sims - row_peak), axis=1, keepdims=True))
    pair_sims = jnp.where(is_pair, sims, MASKED)
    pos_peak = jnp.max(pair_sims, axis=1, keepdims=True)
    row_pos = pos_peak + jnp.log(jnp.sum(jnp.exp(pair_sims - pos_peak), axis=1, keepdims=True))
    col_pos = jnp.sum(jnp.where(is_pair, sims, 0.0), axis=0, keepdims=True)
    half_image, half_text = 0.5 / image_count, 0.5 / text_count
    loss = half_text * jnp.sum(col_lse - col_pos) + half_image * jnp.sum(row_lse - row_pos)
    hit = is_pair.astype(F32)
    grad_sims = (
        half_text * (jnp.exp(sims - col_lse) - hit)
        + half_image * (jnp.exp(sims - row_lse) - jnp.exp(pair_sims - row_pos))
    ).astype(BF16)
    own_rows = lax.dynamic_slice_in_dim(grad_sims, first_image, items, axis=0)
    own_cols = lax.dynamic_slice_in_dim(grad_sims, first_image * captions, text_n, axis=1)
    grad_image = dot(own_rows, all_text) * SIM_SCALE
    grad_text = dot_tn(own_cols, all_image) * SIM_SCALE
    grad_i = (unit_backward(image_raw, grad_image) * (1.0 / NQ)).astype(BF16)
    return loss, grad_i, unit_backward(text_raw, grad_text).astype(BF16)


def shards(
    n_dp, n_mp, hidden_in, image_feats, caption_lengths, pair_image, out_grad, self_qkv, self_out, cross_query,
    cross_kv, cross_out, up_weight, down_weight, vision_proj, text_proj, norm_gain, norm_bias,
):
    me_m = lax.axis_index("mp")
    me_d = lax.axis_index("dp")
    me = me_d * n_mp + me_m
    block_items_n, seq, width = hidden_in.shape
    items = block_items_n // n_mp
    vis_len, vis_width = image_feats.shape[1:]
    captions = caption_lengths.shape[1]
    tokens_n, query_n, text_n = items * seq, items * NQ, items * captions
    rows, lane = self_qkv.shape[1:]
    rows_kv = cross_kv.shape[1]
    pieces = up_weight.shape[1] // lane
    emb = vision_proj.shape[1]
    half_emb = emb // n_mp
    emb_rows = items + text_n
    vis_pad = -(-vis_len // 16) * 16
    tile = 2 * lane
    tiles = n_mp * pieces * lane // tile
    in_chunks = rows % 16 == 0
    fast = in_chunks and n_dp == 16 and n_mp == 2

    def mine(value):
        return lax.dynamic_slice_in_dim(value, me_m * items, items, axis=0)

    lengths = mine(caption_lengths)

    def cut(value):
        return jnp.moveaxis(value.reshape(value.shape[0], -1, lane), 1, 0).reshape(-1, lane)

    vis_half = lax.dynamic_slice_in_dim(vision_proj, me_m * half_emb, half_emb, axis=1)
    txt_half = lax.dynamic_slice_in_dim(text_proj, me_m * half_emb, half_emb, axis=1)
    misc = jnp.concatenate([vis_half, txt_half, jnp.zeros((rows, lane - 2 * half_emb), BF16)], axis=1)
    packed = jnp.concatenate(
        [
            self_qkv.reshape(-1, lane), cross_query, self_out.T, cross_out.T, cut(up_weight), cut(down_weight.T), misc,
            cross_kv.reshape(-1, lane),
        ],
        axis=0,
    )
    n_parts = 7 + 2 * pieces
    gathered = lax.all_gather(packed, ("mp", "dp"), axis=0, tiled=False).reshape(n_mp, n_dp, -1, lane)
    norms = lax.all_gather(jnp.concatenate([norm_gain, norm_bias], axis=0), "dp", axis=1, tiled=True)
    norms = jnp.pad(norms.astype(F32), ((0, 2), (0, 0)))
    all_pairs = lax.all_gather(pair_image, "dp", axis=0, tiled=True)[None, :]

    hidden = mine(hidden_in).reshape(tokens_n, width)
    cotangent = mine(out_grad).reshape(tokens_n, width)
    feats = jnp.pad(mine(image_feats), ((0, 0), (0, vis_pad - vis_len), (0, 0))).reshape(items * vis_pad, vis_width)
    feats_t = feats.T
    feats, feats_t, norms, all_pairs = lax.optimization_barrier((feats, feats_t, norms, all_pairs))

    kv_w = gathered[:, :, n_parts * rows :].reshape(n_mp, n_dp, 2, rows_kv, lane)
    kv_w = jnp.transpose(kv_w, (2, 1, 3, 0, 4)).reshape(2, vis_width, width)
    if in_chunks:
        w, nc, rc = gathered, n_dp, rows
    else:
        w = gathered[:, :, : n_parts * rows].reshape(n_mp, n_dp, n_parts, rows, lane)
        w = jnp.transpose(w, (0, 2, 1, 3, 4)).reshape(n_mp, 1, n_parts * width, lane)
        nc, rc = 1, width

    def vm(*shape, dtype=BF16):
        return pltpu.VMEM(shape, dtype)

    sems = pltpu.SemaphoreType.DMA
    qkv, mixed, resid_one, normed_one, first_query, cross_q = run(
        self_forward,
        [
            ((3, tokens_n, width), BF16), ((tokens_n, width), BF16), ((tokens_n, width), F32), ((tokens_n, width), F32),
            ((query_n, width), BF16), ((query_n, width), BF16),
        ],
        [vm(5, nc, rc, width), sems((5 * n_mp,))],
        ("s", lengths), ("v", hidden), ("v", norms), ("a", w),
    )
    kv, cross_mixed, resid_two, normed_two = run(
        functools.partial(cross_forward, vis_len),
        [
            ((2, items * vis_pad, width), BF16), ((query_n, width), BF16), ((query_n, width), F32),
            ((tokens_n, width), F32),
        ],
        [vm(nc, rc, width), sems((n_mp,))],
        ("v", normed_one), ("v", cross_q), ("v", feats), ("v", kv_w), ("v", norms), ("a", w),
    )
    ffn_scratch = [
        vm(tiles, nc, rc, tile), vm(tiles, nc, rc, tile), vm(n_mp, nc, rc, lane), sems((2 * n_mp * pieces,)), sems((n_mp,)),
    ]
    up_value, act, resid_three, block, cls_rows, image_raw, text_raw, embs = run(
        ffn_forward,
        [
            ((tiles, tokens_n, tile), F32), ((tiles, tokens_n, tile), BF16), ((tokens_n, width), F32),
            ((tokens_n, width), BF16), ((emb_rows, width), BF16), ((emb_rows, emb), F32), ((emb_rows, emb), F32),
            ((emb_rows, emb), BF16),
        ],
        ffn_scratch,
        ("s", lengths), ("v", normed_two), ("v", norms), ("a", w),
    )
    if fast:
        both = ("dp", "mp")
        n_dev = n_dp * n_mp

        def spread(value, steps):
            got = [value] + [lax.ppermute(value, both, [(i, i ^ s) for i in range(n_dev)]) for s in steps]
            return jnp.concatenate(got, axis=0)

        everything = spread(spread(spread(embs, (8, 16, 24)), (4, 1, 5)), (2,))
        loss, grad_i, grad_t = run(
            functools.partial(contrast, items, captions),
            [((1, 1), F32), ((emb_rows, emb), BF16), ((emb_rows, emb), BF16)],
            [],
            ("s", jnp.stack([me])), ("v", everything), ("v", all_pairs), ("v", image_raw), ("v", text_raw),
        )
        loss = loss[0, 0]
    else:
        everything = lax.all_gather(embs, ("dp", "mp"), axis=0, tiled=False)
        all_image, all_text = everything[:, :items].reshape(-1, emb), everything[:, items:].reshape(-1, emb)
        loss, grad_i, grad_t = contrast_plain(
            all_image, all_text, all_pairs, image_raw[:items], text_raw[:text_n], me * items
        )
        grad_i = jnp.pad(grad_i, ((0, emb_rows - items), (0, 0)))
        grad_t = jnp.pad(grad_t, ((0, emb_rows - text_n), (0, 0)))

    place = jnp.zeros((3,), jnp.int32)
    stored = -(-rows_kv // 16) * 16 if in_chunks else vis_width
    rk = rows_kv if in_chunks else vis_width
    grad_two, norm_c, gw_ffn = run(
        ffn_backward,
        [((tokens_n, width), F32), ((2, width), F32), ((n_mp, nc, (1 + 2 * pieces) * rc, lane), BF16)],
        ffn_scratch,
        ("s", lengths), ("s", place), ("v", grad_i), ("v", grad_t), ("v", block), ("v", cls_rows), ("v", cotangent),
        ("v", normed_two), ("v", resid_three), ("v", up_value), ("v", act), ("v", norms), ("a", w),
    )
    grad_one, norm_b, grad_kv, grad_feats, gw_cross = run(
        functools.partial(cross_backward, vis_len, rc),
        [
            ((tokens_n, width), F32), ((2, width), F32), ((2, items * vis_pad, width), BF16),
            ((items * vis_pad, vis_width), BF16), ((n_mp, nc, 2 * rc, lane), BF16),
        ],
        [vm(2, nc, rc, width), vm(query_n, width), sems((2 * n_mp,))],
        ("s", place), ("v", grad_two), ("v", resid_two), ("v", cross_mixed), ("v", cross_q), ("v", first_query),
        ("v", kv), ("v", kv_w), ("v", norms), ("a", w),
    )
    swap = [(i, i ^ 1) for i in range(n_mp)]
    grad_feats = grad_feats.reshape(items, vis_pad, vis_width)[:, :vis_len]
    far_feats = lax.ppermute(grad_feats, "mp", swap)
    (gw_kv,) = run(
        functools.partial(kv_backward, rk, stored),
        [((n_mp, nc, 2 * stored, lane), BF16)],
        [],
        ("s", place), ("v", feats_t), ("v", grad_kv),
    )
    grad_hidden, gw_self = run(
        functools.partial(self_backward, rc),
        [((tokens_n, width), BF16), ((n_mp, nc, 5 * rc, lane), BF16)],
        [vm(4, nc, rc, width), vm(tokens_n, width), vm(3, tokens_n, width), sems((4 * n_mp,))],
        ("s", lengths), ("s", place), ("v", grad_one), ("v", resid_one), ("v", hidden), ("v", mixed), ("v", qkv),
        ("v", norms), ("v", norm_b), ("v", norm_c), ("a", w),
    )

    groups = [(gw_self, 5, rows, rows), (gw_cross, 2, rows, rows), (gw_ffn, 1 + 2 * pieces, rows, rows)]
    groups += [(gw_kv, 2, rows_kv, stored if in_chunks else rows_kv)]
    if not in_chunks:
        groups = [
            (
                jnp.transpose(g.reshape(n_mp, count, n_dp, size, lane), (0, 2, 1, 3, 4)).reshape(n_mp, n_dp, -1, lane),
                count, size, size,
            )
            for g, count, size, _ in groups
        ]
    packed_grad = jnp.concatenate([g for g, *_ in groups], axis=2).reshape(n_mp * n_dp, -1, lane)
    summed = lax.psum_scatter(packed_grad, ("mp", "dp"), scatter_dimension=0, tiled=False).astype(F32)
    parts, at = [], 0
    for _, count, size, kept in groups:
        for _ in range(count):
            parts.append(summed[at : at + size])
            at += kept
    g_qkv, g_out, g_norm, g_cross_out, g_query = parts[:3], parts[3], parts[4], parts[5], parts[6]
    g_up, g_down, g_misc = parts[7 : 7 + pieces], parts[7 + pieces : 7 + 2 * pieces], parts[7 + 2 * pieces]
    g_kv = parts[8 + 2 * pieces :]

    def whole(own, far, axis):
        first = jnp.where(me_m == 0, own, far)
        second = jnp.where(me_m == 0, far, own)
        return jnp.concatenate([first, second], axis=axis)

    def exchanged(value):
        return whole(value, lax.ppermute(value, "mp", swap), 0)

    small = jnp.concatenate([g_misc[:, : 2 * half_emb], g_norm[:, :128]], axis=1).astype(BF16)
    far = lax.ppermute(small, "mp", swap)
    low = jnp.where(me_m == 0, small, far).astype(F32)
    high = jnp.where(me_m == 0, far, small).astype(F32)
    norm_share = low[:, 2 * half_emb : 2 * half_emb + 6].T
    return (
        loss,
        exchanged(block.reshape(items, seq, width)),
        exchanged(grad_hidden.reshape(items, seq, width)),
        whole(grad_feats, far_feats, 0),
        jnp.stack(g_qkv),
        g_out.T,
        g_query,
        jnp.stack(g_kv),
        g_cross_out.T,
        jnp.concatenate(g_up, axis=1),
        jnp.concatenate(g_down, axis=1).T,
        jnp.concatenate([low[:, :half_emb], high[:, :half_emb]], axis=1),
        jnp.concatenate([low[:, half_emb : 2 * half_emb], high[:, half_emb : 2 * half_emb]], axis=1),
        norm_share[:3],
        norm_share[3:],
    )


def solution(mesh):
    n_dp, n_mp = mesh.shape["dp"], mesh.shape["mp"]

    def body(*args):
        return shards(n_dp, n_mp, *args)

    return jax.shard_map(
        body,
        mesh=mesh,
        in_specs=(
            P("dp", None, None),
            P("dp", None, None),
            P("dp", None),
            P("dp"),
            P("dp", None, None),
            P(None, "dp", "mp"),
            P("mp", "dp"),
            P("dp", "mp"),
            P(None, "dp", "mp"),
            P("mp", "dp"),
            P("dp", "mp"),
            P("mp", "dp"),
            P("dp", None),
            P("dp", None),
            P(None, "dp"),
            P(None, "dp"),
        ),
        out_specs=(
            P(),
            P("dp", None, None),
            P("dp", None, None),
            P("dp", None, None),
            P(None, "dp", "mp"),
            P("mp", "dp"),
            P("dp", "mp"),
            P(None, "dp", "mp"),
            P("mp", "dp"),
            P("dp", "mp"),
            P("mp", "dp"),
            P("dp", None),
            P("dp", None),
            P(None, "dp"),
            P(None, "dp"),
        ),
        check_vma=False,
    )
```

```python
import functools

import jax
import jax.numpy as jnp
from jax import lax
from jax.experimental import pallas as pl
from jax.experimental.pallas import tpu as pltpu
from jax.sharding import PartitionSpec as P

HEAD_DIM = 64
NQ = 32
EPS_NORM = 1e-06
EPS_UNIT = 1e-06
SIM_SCALE = 16.0
MASKED = -1000000000.0
F32 = jnp.float32
BF16 = jnp.bfloat16


def dot(left, right):
    return jnp.dot(left, right, preferred_element_type=F32)


def dot_nt(left, right):
    return lax.dot_general(left, right, (((1,), (1,)), ((), ())), preferred_element_type=F32)


def dot_tn(left, right):
    return lax.dot_general(left, right, (((0,), (0,)), ((), ())), preferred_element_type=F32)


def iota(shape, dim):
    return lax.broadcasted_iota(jnp.int32, shape, dim)


def norm_forward(value, gain, shift):
    mean = jnp.mean(value, -1, keepdims=True)
    centered = value - mean
    scale = lax.rsqrt(jnp.mean(centered * centered, -1, keepdims=True) + EPS_NORM)
    return centered * scale * gain + shift


def norm_backward(value, grad, gain):
    mean = jnp.mean(value, -1, keepdims=True)
    centered = value - mean
    scale = lax.rsqrt(jnp.mean(centered * centered, -1, keepdims=True) + EPS_NORM)
    unit = centered * scale
    inner = grad * gain
    back = scale * (inner - jnp.mean(inner, -1, keepdims=True) - unit * jnp.mean(inner * unit, -1, keepdims=True))
    return back, jnp.sum(grad * unit, 0, keepdims=True), jnp.sum(grad, 0, keepdims=True)


def low_lanes(rows):
    return iota((rows, 2 * HEAD_DIM), 1) < HEAD_DIM


def pair_rows(value):
    low = low_lanes(value.shape[0])
    value = value.astype(F32)
    zero = jnp.zeros_like(value)
    return jnp.concatenate([jnp.where(low, value, zero), jnp.where(low, zero, value)], axis=0).astype(BF16)


def merge_rows(value):
    half = value.shape[0] // 2
    return jnp.where(low_lanes(half), value[:half], value[half:])


def probabilities(queries, keys, keep):
    scores = dot_nt(queries, keys) * HEAD_DIM ** (-0.5)
    scores = jnp.where(keep, scores, MASKED)
    expo = jnp.exp(scores - jnp.max(scores, -1, keepdims=True))
    return expo / jnp.sum(expo, -1, keepdims=True)


def attention_back(queries, keys, values, grads, keep):
    probs = probabilities(queries, keys, keep)
    grad_probs = dot_nt(grads, values)
    grad_scores = (probs * (grad_probs - jnp.sum(grad_probs * probs, -1, keepdims=True))).astype(BF16)
    scale = HEAD_DIM ** (-0.5)
    grad_q = merge_rows(dot(grad_scores, keys)) * scale
    grad_k = dot_tn(grad_scores, queries) * scale
    grad_v = dot_tn(probs.astype(BF16), grads)
    return grad_q.astype(BF16), grad_k.astype(BF16), grad_v.astype(BF16)


def same_segment(lens_ref, item, rows, keys):
    first = NQ + lens_ref[item, 0]
    second = first + lens_ref[item, 1]

    def label(place):
        return (
            (place >= NQ).astype(jnp.int32) + (place >= first).astype(jnp.int32) + (place >= second).astype(jnp.int32)
        )

    return label(iota((rows, keys), 0) & (keys - 1)) == label(iota((rows, keys), 1))


def aligned(index, step):
    return pl.ds(pl.multiple_of(index * step, step), step)


def fetch(weights, part, chunk_rows, target, sems, first):
    lane = weights.shape[3]
    copies = []
    for m in range(weights.shape[0]):
        copies.append(
            pltpu.make_async_copy(
                weights.at[m, :, pl.ds(part * chunk_rows, chunk_rows), :],
                target.at[:, :, pl.ds(m * lane, lane)],
                sems.at[first + m],
            )
        )
        copies[-1].start()
    return copies


def fetch_tile(weights, part, chunk_rows, target, lane_at, m, sem):
    lane = weights.shape[3]
    copy = pltpu.make_async_copy(
        weights.at[m, :, pl.ds(part * chunk_rows, chunk_rows), :], target.at[:, :, pl.ds(lane_at, lane)], sem
    )
    copy.start()
    return copy


def flat(ref_value):
    return ref_value.reshape(-1, ref_value.shape[-1])


def share(outs, me_ref, order, row_at, stored, tile_ref, m, lanes, chunk_rows):
    if len(outs) == 1:
        outs[0][m, 0, pl.ds(row_at, stored), :] = tile_ref[pl.ds(0, stored), lanes].astype(BF16)
        return
    for r in range(16):
        rows = pl.ds(pl.multiple_of((me_ref[2] ^ r) * chunk_rows, 8), stored)
        at = {"x": (r >> 1) & 1, "y": me_ref[1] ^ m, "v": (r >> 2) & 1, "u": (r >> 3) & 1}
        i, j, k, n = (at[axis] for axis in order)
        outs[r & 1][i, j, k, n, pl.ds(row_at, stored), :] = tile_ref[rows, lanes].astype(BF16)


def share_halves(outs, me_ref, order, row_at, stored, tile_ref, value, chunk_rows, lane):
    tile_ref[pl.ds(0, value.shape[0]), :] = value
    for m in range(value.shape[1] // lane):
        share(outs, me_ref, order, row_at, stored, tile_ref, m, slice(m * lane, (m + 1) * lane), chunk_rows)


def self_forward(lens_ref, hid_ref, norm_ref, w_ref, qkv_ref, mixed_ref, resid_ref, normed_ref, fq_ref, cq_ref, wbuf, sems):
    items = lens_ref.shape[0]
    seq = hid_ref.shape[0] // items
    width = hid_ref.shape[1]
    rc = wbuf.shape[2]
    copies = [fetch(w_ref, p, rc, wbuf.at[p], sems, p * w_ref.shape[0]) for p in range(5)]
    x = hid_ref[...]
    for j in range(3):
        for c in copies[j]:
            c.wait()
        qkv_ref[j] = dot(x, flat(wbuf[j])).astype(BF16)

    def one(item, carry):
        rows = aligned(item, seq)
        keep = same_segment(lens_ref, item, 2 * seq, seq)
        for p in range(width // 128):
            lanes = pl.ds(p * 128, 128)
            probs = probabilities(pair_rows(qkv_ref[0, rows, lanes]), qkv_ref[1, rows, lanes], keep)
            mixed_ref[rows, lanes] = merge_rows(dot(probs.astype(BF16), qkv_ref[2, rows, lanes])).astype(BF16)
        return carry

    lax.fori_loop(0, items, one, 0)
    for p in (3, 4):
        for c in copies[p]:
            c.wait()
    resid = x.astype(F32) + dot_nt(mixed_ref[...], flat(wbuf[4]))
    resid_ref[...] = resid
    normed = norm_forward(resid, norm_ref[0:1], norm_ref[3:4])
    normed_ref[...] = normed
    query = jnp.concatenate([normed[i * seq : i * seq + NQ] for i in range(items)], axis=0).astype(BF16)
    fq_ref[...] = query
    cq_ref[...] = dot(query, flat(wbuf[3])).astype(BF16)


def cross_forward(
    vis_len, normed_ref, cq_ref, feat_ref, kvw_ref, norm_ref, w_ref, kv_ref, mixed_ref, resid_ref, two_ref, wbuf, sems
):
    items = cq_ref.shape[0] // NQ
    seq = normed_ref.shape[0] // items
    width = cq_ref.shape[1]
    vis_pad = feat_ref.shape[0] // items
    copies = fetch(w_ref, 5, wbuf.shape[1], wbuf, sems, 0)
    step = 256
    for j in range(2):

        def project(n, carry, j=j):
            lanes = aligned(n, step)
            kv_ref[j, :, lanes] = dot(feat_ref[...], kvw_ref[j, :, lanes]).astype(BF16)
            return carry

        lax.fori_loop(0, width // step, project, 0)

    def one(item, carry):
        rows, keys = aligned(item, NQ), aligned(item, vis_pad)
        keep = iota((2 * NQ, vis_pad), 1) < vis_len
        for p in range(width // 128):
            lanes = pl.ds(p * 128, 128)
            probs = probabilities(pair_rows(cq_ref[rows, lanes]), kv_ref[0, keys, lanes], keep)
            mixed_ref[rows, lanes] = merge_rows(dot(probs.astype(BF16), kv_ref[1, keys, lanes])).astype(BF16)
        return carry

    lax.fori_loop(0, items, one, 0)
    for c in copies:
        c.wait()
    first = jnp.concatenate([normed_ref[i * seq : i * seq + NQ] for i in range(items)], axis=0)
    resid = first + dot_nt(mixed_ref[...], flat(wbuf[...]))
    resid_ref[...] = resid
    normed = norm_forward(resid, norm_ref[1:2], norm_ref[4:5])
    for i in range(items):
        two_ref[i * seq : i * seq + NQ] = normed[i * NQ : (i + 1) * NQ]
        two_ref[i * seq + NQ : (i + 1) * seq] = normed_ref[i * seq + NQ : (i + 1) * seq]


def picker_of(lens_ref, rows, seq):
    items, captions = lens_ref.shape
    shape = (rows, items * seq)
    row = iota(shape, 0)
    target = jnp.full(shape, -1, jnp.int32)
    for i in range(items):
        start = i * seq + NQ
        for c in range(captions):
            target = jnp.where(row == i * captions + c, start, target)
            start = start + lens_ref[i, c]
    return (target == iota(shape, 1)).astype(F32).astype(BF16)


def unit_forward(value):
    return value * lax.rsqrt(jnp.sum(value * value, -1, keepdims=True) + EPS_UNIT)


def unit_backward(value, grad):
    scale = lax.rsqrt(jnp.sum(value * value, -1, keepdims=True) + EPS_UNIT)
    return grad * scale - value * (scale * scale * scale * jnp.sum(grad * value, -1, keepdims=True))


def ffn_fetch(w_ref, up_buf, down_buf, sems):
    n_mp, lane = w_ref.shape[0], w_ref.shape[3]
    tiles, _, rc, tile = up_buf.shape
    per = tile // lane
    pieces = tiles * per // n_mp
    ups, downs = [[] for _ in range(tiles)], [[] for _ in range(tiles)]
    for t in range(tiles):
        for s in range(per):
            piece = t * per + s
            m, p = piece // pieces, piece % pieces
            ups[t].append(fetch_tile(w_ref, 6 + p, rc, up_buf.at[t], s * lane, m, sems.at[2 * piece]))
            downs[t].append(fetch_tile(w_ref, 6 + pieces + p, rc, down_buf.at[t], s * lane, m, sems.at[2 * piece + 1]))
    return ups, downs


def misc_fetch(w_ref, part, misc_buf, sems):
    rc = misc_buf.shape[2]
    copies = []
    for m in range(w_ref.shape[0]):
        copies.append(
            pltpu.make_async_copy(w_ref.at[m, :, pl.ds(part * rc, rc), :], misc_buf.at[m], sems.at[m])
        )
        copies[-1].start()
    return copies


def ffn_forward(
    lens_ref, two_ref, norm_ref, w_ref, up_ref, act_ref, resid_ref, block_ref, cls_ref, iraw_ref, traw_ref, emb_ref,
    up_buf, down_buf, misc_buf, sems, msems,
):
    items, captions = lens_ref.shape
    seq = two_ref.shape[0] // items
    tiles = up_buf.shape[0]
    n_mp, lane = w_ref.shape[0], w_ref.shape[3]
    ups, downs = ffn_fetch(w_ref, up_buf, down_buf, sems)
    miscs = misc_fetch(w_ref, 6 + 2 * (tiles * (up_buf.shape[3] // lane) // n_mp), misc_buf, msems)
    two = two_ref[...]
    two_b = two.astype(BF16)
    resid = two
    for t in range(tiles):
        for c in ups[t]:
            c.wait()
        up = dot(two_b, flat(up_buf[t]))
        up_ref[t] = up
        act = (0.5 * up * (1.0 + lax.erf(up * (0.5**0.5)))).astype(BF16)
        act_ref[t] = act
        for c in downs[t]:
            c.wait()
        resid = resid + dot_nt(act, flat(down_buf[t]))
    resid_ref[...] = resid
    block = norm_forward(resid, norm_ref[2:3], norm_ref[5:6]).astype(BF16)
    block_ref[...] = block
    rows = iraw_ref.shape[0]
    cls = dot(picker_of(lens_ref, rows, seq), block).astype(BF16)
    cls_ref[...] = cls
    query = jnp.concatenate([block[i * seq : i * seq + NQ] for i in range(items)], axis=0)
    for c in miscs:
        c.wait()
    half = iraw_ref.shape[1] // n_mp
    row = iota((rows, half), 0)
    for m in range(n_mp):
        misc = flat(misc_buf[m])
        image = dot(query, misc[:, :half])
        raw = jnp.zeros((rows, half), F32)
        for i in range(items):
            raw = jnp.where(row == i, jnp.sum(image[i * NQ : (i + 1) * NQ], 0, keepdims=True) * (1.0 / NQ), raw)
        iraw_ref[:, m * half : (m + 1) * half] = raw
        traw_ref[:, m * half : (m + 1) * half] = dot(cls, misc[:, half : 2 * half])
    image_b = unit_forward(iraw_ref[...]).astype(BF16)
    text_b = unit_forward(traw_ref[...]).astype(BF16)
    r, c = iota((rows, rows), 0), iota((rows, rows), 1)
    put_image = ((r == c) & (r < items)).astype(F32).astype(BF16)
    put_text = ((r == c + items) & (c < items * captions)).astype(F32).astype(BF16)
    emb_ref[...] = (dot(put_image, image_b) + dot(put_text, text_b)).astype(BF16)


def device_of(place, shift, me):
    place = place >> shift
    relative = ((place >> 3) & 1) + 2 * (place >> 4) + 4 * ((place >> 2) & 1) + 8 * (place & 3)
    return relative ^ me


def contrast(items, captions, me_ref, emb_ref, pair_ref, iraw_ref, traw_ref, loss_ref, gi_ref, gt_ref):
    me = me_ref[0]
    rows = iraw_ref.shape[0]
    n_dev = emb_ref.shape[0] // rows
    shift = rows.bit_length() - 1
    images, texts = n_dev * items, n_dev * captions * items
    emb = emb_ref[...]
    r, c = iota((images, n_dev * rows), 0), iota((images, n_dev * rows), 1)
    slot = c & (rows - 1)
    pick = ((device_of(c, shift, me) * items + slot == r) & (slot < items)).astype(F32).astype(BF16)
    image = dot(pick, emb).astype(BF16)
    r, c = iota((texts, n_dev * rows), 0), iota((texts, n_dev * rows), 1)
    slot = (c & (rows - 1)) - items
    pick = ((device_of(c, shift, me) * (items * captions) + slot == r) & (slot >= 0)).astype(F32).astype(BF16)
    text = dot(pick, emb).astype(BF16)
    sims = dot_nt(image, text) * SIM_SCALE
    is_pair = pair_ref[...] == iota((images, texts), 0)
    col_peak = jnp.max(sims, 0, keepdims=True)
    col_lse = col_peak + jnp.log(jnp.sum(jnp.exp(sims - col_peak), 0, keepdims=True))
    row_peak = jnp.max(sims, 1, keepdims=True)
    row_lse = row_peak + jnp.log(jnp.sum(jnp.exp(sims - row_peak), 1, keepdims=True))
    pair_sims = jnp.where(is_pair, sims, MASKED)
    pos_peak = jnp.max(pair_sims, 1, keepdims=True)
    row_pos = pos_peak + jnp.log(jnp.sum(jnp.exp(pair_sims - pos_peak), 1, keepdims=True))
    col_pos = jnp.sum(jnp.where(is_pair, sims, 0.0), 0, keepdims=True)
    half_image, half_text = 0.5 / images, 0.5 / texts
    loss_ref[...] = half_text * jnp.sum(col_lse - col_pos, axis=1, keepdims=True) + half_image * jnp.sum(
        row_lse - row_pos, axis=0, keepdims=True
    )
    hit = jnp.where(is_pair, 1.0, 0.0)
    grad = (
        half_text * (jnp.exp(sims - col_lse) - hit)
        + half_image * (jnp.exp(sims - row_lse) - jnp.exp(pair_sims - row_pos))
    ).astype(BF16)
    r, c = iota((rows, images), 0), iota((rows, images), 1)
    own = ((c == me * items + r) & (r < items)).astype(F32).astype(BF16)
    grad_image = dot(dot(own, grad).astype(BF16), text) * SIM_SCALE
    r, c = iota((rows, texts), 0), iota((rows, texts), 1)
    own = ((c == me * (items * captions) + r) & (r < items * captions)).astype(F32).astype(BF16)
    grad_text = dot(dot_nt(own, grad).astype(BF16), image) * SIM_SCALE
    gi_ref[...] = (unit_backward(iraw_ref[...], grad_image) * (1.0 / NQ)).astype(BF16)
    gt_ref[...] = unit_backward(traw_ref[...], grad_text).astype(BF16)


def ffn_backward(
    orders, lens_ref, me_ref, gi_ref, gt_ref, block_ref, cls_ref, og_ref, two_ref, resid_ref, up_ref, act_ref, norm_ref, w_ref,
    gtwo_ref, ng_ref, *refs,
):
    outs, (up_buf, down_buf, misc_buf, sems, msems, tile_ref) = refs[:-6], refs[-6:]
    downs_out, ups_out = outs[: len(outs) // 2], outs[len(outs) // 2 :]
    items = lens_ref.shape[0]
    seq = two_ref.shape[0] // items
    tokens = two_ref.shape[0]
    tiles, nc, rc, tile = up_buf.shape
    n_mp, lane = w_ref.shape[0], w_ref.shape[3]
    per = tile // lane
    pieces = tiles * per // n_mp
    miscs = misc_fetch(w_ref, 6 + 2 * pieces, misc_buf, msems)
    ups, downs = ffn_fetch(w_ref, up_buf, down_buf, sems)
    rows, emb = gi_ref.shape
    half = emb // n_mp
    gi, gt = gi_ref[...], gt_ref[...]
    r, c = iota((tokens, rows), 0), iota((tokens, rows), 1)
    spread = (((r // seq) == c) & ((r & (seq - 1)) < NQ)).astype(F32).astype(BF16)
    gi_rows = dot(spread, gi).astype(BF16)
    gt_rows = dot_tn(picker_of(lens_ref, rows, seq), gt).astype(BF16)
    for c in miscs:
        c.wait()
    grad = og_ref[...].astype(F32)
    block = block_ref[...]
    cls = cls_ref[...]
    zero = jnp.zeros((rc * nc, lane - 2 * half), F32)
    for m in range(n_mp):
        misc = flat(misc_buf[m])
        lanes = slice(m * half, (m + 1) * half)
        grad = grad + dot_nt(gi_rows[:, lanes], misc[:, :half]) + dot_nt(gt_rows[:, lanes], misc[:, half : 2 * half])
        tile_ref[:, :lane] = jnp.concatenate([dot_tn(block, gi_rows[:, lanes]), dot_tn(cls, gt[:, lanes]), zero], axis=1)
        share(ups_out, me_ref, orders[1], pieces * rc, rc, tile_ref, m, slice(0, lane), rc)
    back, gain_grad, shift_grad = norm_backward(resid_ref[...], grad, norm_ref[2:3])
    ng_ref[...] = jnp.concatenate([gain_grad, shift_grad], axis=0)
    branch = back.astype(BF16)
    two_b = two_ref[...].astype(BF16)
    total = back
    for t in range(tiles):
        for c in downs[t] + ups[t]:
            c.wait()
        up = up_ref[t]
        slope = 0.5 * (1.0 + lax.erf(up * (0.5**0.5))) + up * jnp.exp(-0.5 * up * up) * 0.3989422804014327
        grad_up = (dot(branch, flat(down_buf[t])) * slope).astype(BF16)
        m, p = (t * per) // pieces, (t * per) % pieces
        for outs, order, left, right in (
            (ups_out, orders[1], two_b, grad_up), (downs_out, orders[0], branch, act_ref[t])
        ):
            tile_ref[...] = dot_tn(left, right)
            for s in range(per):
                share(outs, me_ref, order, (p + s) * rc, rc, tile_ref, m, slice(s * lane, (s + 1) * lane), rc)
        total = total + dot_nt(grad_up, flat(up_buf[t]))
    gtwo_ref[...] = total


def cross_backward(
    vis_len, gtwo_ref, resid_ref, cq_ref, kv_ref, norm_ref, w_ref, gone_ref, ng_ref, gkv_ref, gq_ref, branch_ref, wbuf, sems,
):
    items = cq_ref.shape[0] // NQ
    seq = gtwo_ref.shape[0] // items
    width = cq_ref.shape[1]
    vis_pad = kv_ref.shape[1] // items
    n_mp = w_ref.shape[0]
    copies = [fetch(w_ref, p, wbuf.shape[2], wbuf.at[i], sems, i * n_mp) for i, p in enumerate((5, 3))]
    grad = jnp.concatenate([gtwo_ref[i * seq : i * seq + NQ] for i in range(items)], axis=0)
    back, gain_grad, shift_grad = norm_backward(resid_ref[...], grad, norm_ref[1:2])
    ng_ref[...] = jnp.concatenate([gain_grad, shift_grad], axis=0)
    branch = back.astype(BF16)
    branch_ref[...] = branch
    for c in copies[0]:
        c.wait()
    gq_ref[...] = dot(branch, flat(wbuf[0])).astype(BF16)

    def one(item, carry):
        rows, keys = aligned(item, NQ), aligned(item, vis_pad)
        keep = iota((2 * NQ, vis_pad), 1) < vis_len
        for p in range(width // 128):
            lanes = pl.ds(p * 128, 128)
            grad_q, grad_k, grad_v = attention_back(
                pair_rows(cq_ref[rows, lanes]), kv_ref[0, keys, lanes], kv_ref[1, keys, lanes],
                pair_rows(gq_ref[rows, lanes]), keep,
            )
            gq_ref[rows, lanes] = grad_q
            gkv_ref[0, keys, lanes] = grad_k
            gkv_ref[1, keys, lanes] = grad_v
        return carry

    lax.fori_loop(0, items, one, 0)
    for c in copies[1]:
        c.wait()
    first = back + dot_nt(gq_ref[...], flat(wbuf[1]))
    for i in range(items):
        gone_ref[i * seq : i * seq + NQ] = first[i * NQ : (i + 1) * NQ]
        gone_ref[i * seq + NQ : (i + 1) * seq] = gtwo_ref[i * seq + NQ : (i + 1) * seq]


def feats_backward(gkv_ref, kvw_ref, gf_ref):
    step = 128

    def feats(n, carry):
        lanes = aligned(n, step)
        total = dot_nt(gkv_ref[0], kvw_ref[0, lanes, :]) + dot_nt(gkv_ref[1], kvw_ref[1, lanes, :])
        gf_ref[:, lanes] = total.astype(BF16)
        return carry

    lax.fori_loop(0, gf_ref.shape[1] // step, feats, 0)


def cross_weights_backward(
    rc, rk, stored, lane, order, me_ref, feat_t_ref, gkv_ref, branch_ref, mixed_ref, fq_ref, gq_ref, *refs,
):
    outs, tile_ref = refs[:-1], refs[-1]
    share_halves(outs, me_ref, order, 0, rc, tile_ref, dot_tn(branch_ref[...], mixed_ref[...]), rc, lane)
    share_halves(outs, me_ref, order, rc, rc, tile_ref, dot_tn(fq_ref[...], gq_ref[...]), rc, lane)
    for j in range(2):
        grad = dot(feat_t_ref[...], gkv_ref[j])
        share_halves(outs, me_ref, order, 2 * rc + j * stored, stored, tile_ref, grad, rk, lane)


def self_attention_backward(
    lens_ref, gone_ref, resid_ref, qkv_ref, norm_ref, w_ref, back_ref, ng_ref, gqkv_ref, wbuf, gm_buf, sems,
):
    items = lens_ref.shape[0]
    seq = gone_ref.shape[0] // items
    width = gone_ref.shape[1]
    copies = fetch(w_ref, 4, wbuf.shape[1], wbuf, sems, 0)
    back, gain_grad, shift_grad = norm_backward(resid_ref[...], gone_ref[...], norm_ref[0:1])
    back_ref[...] = back
    ng_ref[...] = jnp.concatenate([gain_grad, shift_grad], axis=0)
    for c in copies:
        c.wait()
    gm_buf[...] = dot(back.astype(BF16), flat(wbuf[...])).astype(BF16)

    def one(item, carry):
        rows = aligned(item, seq)
        keep = same_segment(lens_ref, item, 2 * seq, seq)
        for p in range(width // 128):
            lanes = pl.ds(p * 128, 128)
            grads = attention_back(
                pair_rows(qkv_ref[0, rows, lanes]), qkv_ref[1, rows, lanes], qkv_ref[2, rows, lanes],
                pair_rows(gm_buf[rows, lanes]), keep,
            )
            for j in range(3):
                gqkv_ref[j, rows, lanes] = grads[j]
        return carry

    lax.fori_loop(0, items, one, 0)


def self_weights_backward(
    rc, order, me_ref, back_ref, hid_ref, mixed_ref, gqkv_ref, nga_ref, ngb_ref, ngc_ref, w_ref, gh_ref, *refs,
):
    outs, (wbuf, sems, tile_ref) = refs[:-3], refs[-3:]
    width = hid_ref.shape[1]
    n_mp, lane = w_ref.shape[0], w_ref.shape[3]
    copies = [fetch(w_ref, p, wbuf.shape[2], wbuf.at[p], sems, p * n_mp) for p in range(3)]
    x = hid_ref[...]
    for j in range(3):
        share_halves(outs, me_ref, order, j * rc, rc, tile_ref, dot_tn(x, gqkv_ref[j]), rc, lane)
    branch = back_ref[...].astype(BF16)
    share_halves(outs, me_ref, order, 3 * rc, rc, tile_ref, dot_tn(branch, mixed_ref[...]), rc, lane)
    norms = jnp.concatenate(
        [r[0:1] for r in (nga_ref, ngb_ref, ngc_ref)] + [r[1:2] for r in (nga_ref, ngb_ref, ngc_ref)]
        + [jnp.zeros((122, width), F32)],
        axis=0,
    ).T
    tile_ref[:, :lane] = jnp.concatenate([norms, jnp.zeros((width, lane - 128), F32)], axis=1)
    for m in range(n_mp):
        share(outs, me_ref, order, 4 * rc, rc, tile_ref, m, slice(0, lane), rc)
    total = back_ref[...]
    for j in range(3):
        for c in copies[j]:
            c.wait()
        total = total + dot_nt(gqkv_ref[j], flat(wbuf[j]))
    gh_ref[...] = total.astype(BF16)


def run(body, outs, scratch, *ins, after=()):
    spaces = {"v": pltpu.VMEM, "s": pltpu.SMEM, "a": pl.ANY}

    def kernel(*refs):
        body(*refs[: len(ins)], *refs[len(ins) + len(after) :])

    def spec(kind, value):
        if kind == "f":
            return pl.BlockSpec((1, *value.shape[1:]), lambda i: (0, 0, 0))
        return pl.BlockSpec(memory_space=spaces[kind])

    grid = {"grid": (1,)} if any(kind == "f" for kind, _ in ins) else {}
    return pl.pallas_call(
        kernel,
        **grid,
        out_shape=[jax.ShapeDtypeStruct(shape, dtype) for shape, dtype in outs],
        in_specs=[spec(kind, value) for kind, value in ins] + [pl.BlockSpec(memory_space=pl.ANY)] * len(after),
        out_specs=[pl.BlockSpec(memory_space=pltpu.VMEM) for _ in outs],
        scratch_shapes=scratch,
        cost_estimate=pl.CostEstimate(flops=3 * 10**10, bytes_accessed=10**8, transcendentals=0),
        compiler_params=pltpu.CompilerParams(vmem_limit_bytes=60 * 1024 * 1024),
    )(*[value for _, value in ins], *after)


def combine(terms, after):
    left = min(t.ndim for t in terms) - 2
    places = 2 ** (left - 1)
    rows, lane = terms[0].shape[-2:]
    terms = [t.reshape(-1, 2, places, rows, lane) for t in terms]

    def kernel(*refs):
        total = refs[0][0, 0, 0].astype(F32)
        for ref in refs[1 : len(terms)]:
            total = total + ref[0, 0, 0].astype(F32)
        refs[-1][0] = total.astype(BF16)

    return pl.pallas_call(
        kernel,
        grid=(places,),
        out_shape=jax.ShapeDtypeStruct((places, rows, lane), BF16),
        in_specs=[pl.BlockSpec((1, 1, 1, rows, lane), lambda i: (0, 1, i, 0, 0))] * len(terms)
        + [pl.BlockSpec(memory_space=pl.ANY)] * len(after),
        out_specs=pl.BlockSpec((1, rows, lane), lambda i: (i, 0, 0)),
        cost_estimate=pl.CostEstimate(flops=3 * 10**10, bytes_accessed=10**8, transcendentals=0),
        compiler_params=pltpu.CompilerParams(vmem_limit_bytes=60 * 1024 * 1024),
    )(*terms, *after).reshape(*(2,) * (left - 1), rows, lane)


def add_terms(refs):
    total = refs[0][0].astype(F32)
    for ref in refs[1:]:
        total = total + ref[0].astype(F32)
    return total


def finish_up(pieces, me_ref, *refs):
    total = add_terms(refs[:-3])
    up_ref, misc_ref, half_ref = refs[-3:]
    half_ref[...] = jnp.full(half_ref.shape, me_ref[1], jnp.int32)
    rows, lane = misc_ref.shape[0], up_ref.shape[1] // pieces
    for p in range(pieces):
        up_ref[:, p * lane : (p + 1) * lane] = total[p * rows : (p + 1) * rows]
    misc_ref[...] = total[pieces * rows :, : misc_ref.shape[1]].astype(BF16)


def finish_rest(pieces, counts, stored, me_ref, misc_ref, far_ref, *refs):
    terms, at = [], 0
    for count in counts:
        terms.append(add_terms(refs[at : at + count]))
        at += count
    down, cross, own = terms
    (
        down_ref, cross_out_ref, query_ref, kv_ref, qkv_ref, out_ref, vision_ref, text_ref, gain_ref, bias_ref,
    ) = refs[at:]
    rows, lane = query_ref.shape
    for p in range(pieces):
        down_ref[:, p * lane : (p + 1) * lane] = down[p * rows : (p + 1) * rows]
    cross_out_ref[...] = cross[:rows]
    query_ref[...] = cross[rows : 2 * rows]
    for j in range(2):
        at = 2 * rows + j * stored
        kv_ref[j] = cross[at : at + kv_ref.shape[1]]
    for j in range(3):
        qkv_ref[j] = own[j * rows : (j + 1) * rows]
    out_ref[...] = own[3 * rows : 4 * rows]
    norms = jnp.concatenate([own[4 * rows : 5 * rows, :128], jnp.zeros((128 - rows, 128), F32)], axis=0).T
    gain_ref[...] = norms[0:3, :rows]
    bias_ref[...] = norms[3:6, :rows]
    half = misc_ref.shape[1] // 2
    near, far = misc_ref[...].astype(F32), far_ref[...].astype(F32)
    first = jnp.full(near.shape, me_ref[1], jnp.int32) == 0
    low, high = jnp.where(first, near, far), jnp.where(first, far, near)
    vision_ref[:, :half] = low[:, :half]
    vision_ref[:, half:] = high[:, :half]
    text_ref[:, :half] = low[:, half:]
    text_ref[:, half:] = high[:, half:]


def contrast_plain(all_image, all_text, all_pairs, image_raw, text_raw, first_image):
    items, text_n = image_raw.shape[0], text_raw.shape[0]
    captions = text_n // items
    image_count, text_count = all_image.shape[0], all_text.shape[0]
    sims = dot_nt(all_image, all_text) * SIM_SCALE
    is_pair = all_pairs == jnp.arange(image_count, dtype=jnp.int32)[:, None]
    col_peak = jnp.max(sims, axis=0, keepdims=True)
    col_lse = col_peak + jnp.log(jnp.sum(jnp.exp(sims - col_peak), axis=0, keepdims=True))
    row_peak = jnp.max(sims, axis=1, keepdims=True)
    row_lse = row_peak + jnp.log(jnp.sum(jnp.exp(sims - row_peak), axis=1, keepdims=True))
    pair_sims = jnp.where(is_pair, sims, MASKED)
    pos_peak = jnp.max(pair_sims, axis=1, keepdims=True)
    row_pos = pos_peak + jnp.log(jnp.sum(jnp.exp(pair_sims - pos_peak), axis=1, keepdims=True))
    col_pos = jnp.sum(jnp.where(is_pair, sims, 0.0), axis=0, keepdims=True)
    half_image, half_text = 0.5 / image_count, 0.5 / text_count
    loss = half_text * jnp.sum(col_lse - col_pos) + half_image * jnp.sum(row_lse - row_pos)
    hit = is_pair.astype(F32)
    grad_sims = (
        half_text * (jnp.exp(sims - col_lse) - hit)
        + half_image * (jnp.exp(sims - row_lse) - jnp.exp(pair_sims - row_pos))
    ).astype(BF16)
    own_rows = lax.dynamic_slice_in_dim(grad_sims, first_image, items, axis=0)
    own_cols = lax.dynamic_slice_in_dim(grad_sims, first_image * captions, text_n, axis=1)
    grad_image = dot(own_rows, all_text) * SIM_SCALE
    grad_text = dot_tn(own_cols, all_image) * SIM_SCALE
    grad_i = (unit_backward(image_raw, grad_image) * (1.0 / NQ)).astype(BF16)
    return loss, grad_i, unit_backward(text_raw, grad_text).astype(BF16)


def shards(
    n_dp, n_mp, hidden_in, image_feats, caption_lengths, pair_image, out_grad, self_qkv, self_out, cross_query,
    cross_kv, cross_out, up_weight, down_weight, vision_proj, text_proj, norm_gain, norm_bias,
):
    me_m = lax.axis_index("mp")
    me_d = lax.axis_index("dp")
    me = me_d * n_mp + me_m
    block_items_n, seq, width = hidden_in.shape
    items = block_items_n // n_mp
    vis_len, vis_width = image_feats.shape[1:]
    captions = caption_lengths.shape[1]
    tokens_n, query_n, text_n = items * seq, items * NQ, items * captions
    rows, lane = self_qkv.shape[1:]
    rows_kv = cross_kv.shape[1]
    pieces = up_weight.shape[1] // lane
    emb = vision_proj.shape[1]
    half_emb = emb // n_mp
    emb_rows = items + text_n
    vis_pad = -(-vis_len // 16) * 16
    tile = 2 * lane
    tiles = n_mp * pieces * lane // tile
    in_chunks = rows % 16 == 0
    fast = in_chunks and n_dp == 16 and n_mp == 2

    def mine(value):
        return lax.dynamic_slice_in_dim(value, me_m * items, items, axis=0)

    lengths = mine(caption_lengths)

    def cut(value):
        return jnp.moveaxis(value.reshape(value.shape[0], -1, lane), 1, 0).reshape(-1, lane)

    vis_half = lax.dynamic_slice_in_dim(vision_proj, me_m * half_emb, half_emb, axis=1)
    txt_half = lax.dynamic_slice_in_dim(text_proj, me_m * half_emb, half_emb, axis=1)
    misc = jnp.concatenate([vis_half, txt_half, jnp.zeros((rows, lane - 2 * half_emb), BF16)], axis=1)
    packed = jnp.concatenate(
        [
            self_qkv.reshape(-1, lane), cross_query, self_out.T, cross_out.T, cut(up_weight), cut(down_weight.T), misc,
            cross_kv.reshape(-1, lane),
        ],
        axis=0,
    )
    n_parts = 7 + 2 * pieces
    gathered = lax.all_gather(packed, ("mp", "dp"), axis=0, tiled=False).reshape(n_mp, n_dp, -1, lane)
    norms = lax.all_gather(jnp.concatenate([norm_gain, norm_bias], axis=0), "dp", axis=1, tiled=True)
    norms = jnp.pad(norms.astype(F32), ((0, 2), (0, 0)))
    all_pairs = lax.all_gather(pair_image, "dp", axis=0, tiled=True)[None, :]

    hidden = mine(hidden_in).reshape(tokens_n, width)
    cotangent = mine(out_grad).reshape(tokens_n, width)
    feats = jnp.pad(mine(image_feats), ((0, 0), (0, vis_pad - vis_len), (0, 0))).reshape(items * vis_pad, vis_width)
    feats_t = feats.T
    feats, feats_t, norms, all_pairs = lax.optimization_barrier((feats, feats_t, norms, all_pairs))

    kv_w = gathered[:, :, n_parts * rows :].reshape(n_mp, n_dp, 2, rows_kv, lane)
    kv_w = jnp.transpose(kv_w, (2, 1, 3, 0, 4)).reshape(2, vis_width, width)
    if in_chunks:
        w, nc, rc = gathered, n_dp, rows
    else:
        w = gathered[:, :, : n_parts * rows].reshape(n_mp, n_dp, n_parts, rows, lane)
        w = jnp.transpose(w, (0, 2, 1, 3, 4)).reshape(n_mp, 1, n_parts * width, lane)
        nc, rc = 1, width

    def vm(*shape, dtype=BF16):
        return pltpu.VMEM(shape, dtype)

    sems = pltpu.SemaphoreType.DMA
    qkv, mixed, resid_one, normed_one, first_query, cross_q = run(
        self_forward,
        [
            ((3, tokens_n, width), BF16), ((tokens_n, width), BF16), ((tokens_n, width), F32), ((tokens_n, width), F32),
            ((query_n, width), BF16), ((query_n, width), BF16),
        ],
        [vm(5, nc, rc, width), sems((5 * n_mp,))],
        ("s", lengths), ("v", hidden), ("v", norms), ("a", w),
    )
    kv, cross_mixed, resid_two, normed_two = run(
        functools.partial(cross_forward, vis_len),
        [
            ((2, items * vis_pad, width), BF16), ((query_n, width), BF16), ((query_n, width), F32),
            ((tokens_n, width), F32),
        ],
        [vm(nc, rc, width), sems((n_mp,))],
        ("v", normed_one), ("v", cross_q), ("v", feats), ("v", kv_w), ("v", norms), ("a", w),
    )
    ffn_scratch = [
        vm(tiles, nc, rc, tile), vm(tiles, nc, rc, tile), vm(n_mp, nc, rc, lane), sems((2 * n_mp * pieces,)), sems((n_mp,)),
    ]
    up_value, act, resid_three, block, cls_rows, image_raw, text_raw, embs = run(
        ffn_forward,
        [
            ((tiles, tokens_n, tile), F32), ((tiles, tokens_n, tile), BF16), ((tokens_n, width), F32),
            ((tokens_n, width), BF16), ((emb_rows, width), BF16), ((emb_rows, emb), F32), ((emb_rows, emb), F32),
            ((emb_rows, emb), BF16),
        ],
        ffn_scratch,
        ("s", lengths), ("v", normed_two), ("v", norms), ("a", w),
    )
    if fast:
        both = ("dp", "mp")
        n_dev = n_dp * n_mp

        def spread(value, steps):
            got = [value] + [lax.ppermute(value, both, [(i, i ^ s) for i in range(n_dev)]) for s in steps]
            return jnp.concatenate(got, axis=0)

        everything = spread(spread(spread(embs, (8, 16, 24)), (4, 1, 5)), (2,))
        loss, grad_i, grad_t = run(
            functools.partial(contrast, items, captions),
            [((1, 1), F32), ((emb_rows, emb), BF16), ((emb_rows, emb), BF16)],
            [],
            ("s", jnp.stack([me])), ("v", everything), ("v", all_pairs), ("v", image_raw), ("v", text_raw),
        )
        loss = loss[0, 0]
    else:
        everything = lax.all_gather(embs, ("dp", "mp"), axis=0, tiled=False)
        all_image, all_text = everything[:, :items].reshape(-1, emb), everything[:, items:].reshape(-1, emb)
        loss, grad_i, grad_t = contrast_plain(
            all_image, all_text, all_pairs, image_raw[:items], text_raw[:text_n], me * items
        )
        grad_i = jnp.pad(grad_i, ((0, emb_rows - items), (0, 0)))
        grad_t = jnp.pad(grad_t, ((0, emb_rows - text_n), (0, 0)))

    place = jnp.stack([me, me_m, me_d])
    stored = -(-rows_kv // 16) * 16 if in_chunks else vis_width
    rk = rows_kv if in_chunks else vis_width
    swap = [(i, i ^ 1) for i in range(n_mp)]

    def shared(rows_n):
        if fast:
            return [((2, 2, 2, 2, rows_n, lane), BF16)] * 2
        return [((n_mp, 1, rows_n, lane), BF16)]

    def along_dp(value, step):
        return lax.ppermute(value, "dp", [(i, i ^ step) for i in range(n_dp)])

    class Sum:
        def __init__(self, order, arrays):
            self.order = order
            if fast:
                keep, send = arrays
                self.terms = [keep, along_dp(send, 1)]

        def step(self, after):
            axis, self.order = self.order[0], self.order[1:]
            sent = combine(self.terms, after)
            if axis == "y":
                self.terms.append(lax.ppermute(sent, "mp", swap))
            else:
                self.terms.append(along_dp(sent, {"x": 2, "v": 4, "u": 8}[axis]))
            return [sent]

        def parts(self):
            return [("f", t.reshape(-1, *t.shape[-2:])) for t in self.terms]

    order_up, order_down, order_cross, order_self = "xvyu", "vxyu", "xvyu", "vxyu"
    grad_two, norm_c, *out_ffn = run(
        functools.partial(ffn_backward, (order_down, order_up)),
        [((tokens_n, width), F32), ((2, width), F32)] + shared(pieces * rc) + shared((pieces + 1) * rc),
        ffn_scratch + [vm(width, tile, dtype=F32)],
        ("s", lengths), ("s", place), ("v", grad_i), ("v", grad_t), ("v", block), ("v", cls_rows), ("v", cotangent),
        ("v", normed_two), ("v", resid_three), ("v", up_value), ("v", act), ("v", norms), ("a", w),
    )
    half_ffn = len(out_ffn) // 2
    out_down, out_up = out_ffn[:half_ffn], out_ffn[half_ffn:]
    sum_down, sum_up = Sum(order_down, out_down), Sum(order_up, out_up)
    far_block = lax.ppermute(block, "mp", swap)
    last = [out_up[0]]

    def steps(*sums):
        nonlocal last
        if fast:
            for each in sums:
                last = each.step(last)

    grad_one, norm_b, grad_kv, grad_cq, branch_two = run(
        functools.partial(cross_backward, vis_len),
        [
            ((tokens_n, width), F32), ((2, width), F32), ((2, items * vis_pad, width), BF16), ((query_n, width), BF16),
            ((query_n, width), BF16),
        ],
        [vm(2, nc, rc, width), sems((2 * n_mp,))],
        ("v", grad_two), ("v", resid_two), ("v", cross_q), ("v", kv), ("v", norms), ("a", w), after=last + [far_block],
    )
    last = [branch_two]
    steps(sum_down, sum_up)
    (grad_feats,) = run(
        feats_backward, [((items * vis_pad, vis_width), BF16)], [], ("v", grad_kv), ("v", kv_w), after=last
    )
    last = [grad_feats]
    far_feats = lax.ppermute(grad_feats, "mp", swap)
    out_cross = run(
        functools.partial(cross_weights_backward, rc, rk, stored, lane, order_cross),
        shared(2 * rc + 2 * stored),
        [vm(vis_width + stored - rk, width, dtype=F32)],
        ("s", place), ("v", feats_t), ("v", grad_kv), ("v", branch_two), ("v", cross_mixed), ("v", first_query),
        ("v", grad_cq), after=last,
    )
    last = [out_cross[0]]
    sum_cross = Sum(order_cross, out_cross)
    steps(sum_down, sum_up)
    grad_resid_one, norm_a, grad_qkv = run(
        self_attention_backward,
        [((tokens_n, width), F32), ((2, width), F32), ((3, tokens_n, width), BF16)],
        [vm(nc, rc, width), vm(tokens_n, width), sems((n_mp,))],
        ("s", lengths), ("v", grad_one), ("v", resid_one), ("v", qkv), ("v", norms), ("a", w), after=last,
    )
    last = [grad_qkv]
    steps(sum_cross)
    grad_hidden, *out_self = run(
        functools.partial(self_weights_backward, rc, order_self),
        [((tokens_n, width), BF16)] + shared(5 * rc),
        [vm(3, nc, rc, width), sems((3 * n_mp,)), vm(width, width, dtype=F32)],
        ("s", place), ("v", grad_resid_one), ("v", hidden), ("v", mixed), ("v", grad_qkv), ("v", norm_a),
        ("v", norm_b), ("v", norm_c), ("a", w), after=last,
    )
    last = [out_self[0]]
    sum_self = Sum(order_self, out_self)
    far_hidden = lax.ppermute(grad_hidden, "mp", swap)
    steps(sum_down, sum_up, sum_self, sum_down, sum_up, sum_cross, sum_self)
    groups = [(out_up, pieces + 1, rows), (out_down, pieces, rows), (out_cross, 2, rows), (out_cross, 2, rows_kv)]
    groups += [(out_self, 5, rows)]

    def whole(own, far, half):
        return jnp.concatenate([jnp.where(half == 0, own, far), jnp.where(half == 0, far, own)], axis=0)


    if fast:
        up_grad, misc, half_late = run(
            functools.partial(finish_up, pieces),
            [((rows, pieces * lane), F32), ((rows, 2 * half_emb), BF16), ((1, 1), jnp.int32)], [],
            ("s", place), *sum_up.parts(), after=last,
        )
        half_late = half_late[0, 0]
        last = [misc]
        far_misc = lax.ppermute(misc, "mp", swap)
        steps(sum_cross, sum_self, sum_cross, sum_self)
        others = [sum_down, sum_cross, sum_self]
        down_grad, cross_out_grad, query_grad, kv_grad, qkv_grad, out_grad_t, vision_grad, text_grad, gain, bias = run(
            functools.partial(finish_rest, pieces, [len(s.terms) for s in others], stored),
            [
                ((rows, pieces * lane), F32), ((rows, lane), F32), ((rows, lane), F32), ((2, rows_kv, lane), F32),
                ((3, rows, lane), F32), ((rows, lane), F32), ((rows, emb), F32), ((rows, emb), F32), ((3, rows), F32),
                ((3, rows), F32),
            ],
            [],
            ("s", place), ("v", misc), ("v", far_misc), *[p for s in others for p in s.parts()],
        )
    else:
        half_late = me_m
        shares, at = [], {}
        for g, count, size in groups:
            start = at.get(id(g), 0)
            at[id(g)] = start + count * n_dp * size
            value = g[0][:, :, start : at[id(g)]].reshape(n_mp, count, n_dp, size, lane)
            shares.append(jnp.transpose(value, (0, 2, 1, 3, 4)).reshape(n_mp * n_dp, -1, lane))
        packed_grad = jnp.concatenate(shares, axis=1)
        got, at = lax.psum_scatter(packed_grad, ("mp", "dp"), scatter_dimension=0, tiled=False).astype(F32), 0
        parts = []
        for _, count, size in groups:
            for _ in range(count):
                parts.append(got[at : at + size])
                at += size
        up_grad = jnp.concatenate(parts[:pieces], axis=1)
        down_grad = jnp.concatenate(parts[pieces + 1 : 2 * pieces + 1], axis=1)
        cross_out_grad, query_grad, *kv_grad = parts[2 * pieces + 1 : 2 * pieces + 5]
        kv_grad, qkv_grad = jnp.stack(kv_grad), jnp.stack(parts[2 * pieces + 5 : 2 * pieces + 8])
        out_grad_t, norm_grad = parts[2 * pieces + 8][:, :], parts[2 * pieces + 9][:, :6].T
        gain, bias = norm_grad[:3], norm_grad[3:]
        misc = parts[pieces][:, : 2 * half_emb].astype(BF16)
        far = lax.ppermute(misc, "mp", swap)
        low = jnp.where(me_m == 0, misc, far).astype(F32)
        high = jnp.where(me_m == 0, far, misc).astype(F32)
        vision_grad = jnp.concatenate([low[:, :half_emb], high[:, :half_emb]], axis=1)
        text_grad = jnp.concatenate([low[:, half_emb:], high[:, half_emb:]], axis=1)
    return (
        loss,
        whole(block.reshape(items, seq, width), far_block.reshape(items, seq, width), half_late),
        whole(grad_hidden.reshape(items, seq, width), far_hidden.reshape(items, seq, width), half_late),
        whole(grad_feats, far_feats, half_late).reshape(-1, vis_pad, vis_width)[:, :vis_len],
        qkv_grad,
        out_grad_t.T,
        query_grad,
        kv_grad,
        cross_out_grad.T,
        up_grad,
        down_grad.T,
        vision_grad,
        text_grad,
        gain,
        bias,
    )


def solution(mesh):
    n_dp, n_mp = mesh.shape["dp"], mesh.shape["mp"]

    def body(*args):
        return shards(n_dp, n_mp, *args)

    return jax.shard_map(
        body,
        mesh=mesh,
        in_specs=(
            P("dp", None, None),
            P("dp", None, None),
            P("dp", None),
            P("dp"),
            P("dp", None, None),
            P(None, "dp", "mp"),
            P("mp", "dp"),
            P("dp", "mp"),
            P(None, "dp", "mp"),
            P("mp", "dp"),
            P("dp", "mp"),
            P("mp", "dp"),
            P("dp", None),
            P("dp", None),
            P(None, "dp"),
            P(None, "dp"),
        ),
        out_specs=(
            P(),
            P("dp", None, None),
            P("dp", None, None),
            P("dp", None, None),
            P(None, "dp", "mp"),
            P("mp", "dp"),
            P("dp", "mp"),
            P(None, "dp", "mp"),
            P("mp", "dp"),
            P("dp", "mp"),
            P("mp", "dp"),
            P("dp", None),
            P("dp", None),
            P(None, "dp"),
            P(None, "dp"),
        ),
        check_vma=False,
    )
```
